512 devices in a mesh: gz: 64 (over z, x), strip: 8 (over y, core).
Axes of the slice: x: 4, y: 4, z: 16, core: 2. Of those that a mesh axis runs over, the one named last changes fastest.
Arguments:
- positions: float32 [64, 2, 256, 640], P('gz', None, 'strip'), may hold values from -3 to 3
- velocity: float32 [64, 2, 256, 640], P('gz', None, 'strip'), may hold values from -3.6 to 3.6
- flow_down: float32 [64, 2, 256, 640], P('gz', None, 'strip'), may hold values from 0 to 1
- flow_up: float32 [64, 2, 256, 640], P('gz', None, 'strip'), may hold values from 0 to 1
- flow_mask: int32 [2, 64, 256, 640], P(None, 'gz', 'strip'), may hold values 0 or 1
- resets: int32 [3, 64], P(None, 'gz'), may hold values 0 or 1
- dt_index: int32 [3], replicated, may hold values from 0 to 4
Outputs:
- final_positions: float32 [64, 2, 256, 640], P('gz', None, 'strip')
- final_velocity: float32 [64, 2, 256, 640], P('gz', None, 'strip')
The draws below stay inside these ranges and needn't reach their ends.
All inputs are finite; a program needn't handle non-finite values. No bound on the sum of `flow_mask` or of `resets` on one device may be relied on, other than what follows from the above.
Results may differ from the reference program's by a relative error of at most 0.0003.
Values sent between devices are 32-bit elements; how exact they have to be, the bound alone decides.
No kernel may reach another device: no remote copies, remote signals or barrier semaphores. Data moves between devices by JAX's collectives and lax.ppermute only.
A program may use at most 64 MiB of HBM per device.

```python
import math
import jax
import jax.numpy as jnp

COLS = 640
STEPS = 3
SECTIONS = 64
NROWS = 256


def draw_velocity(key, part):
    key = jax.random.fold_in(key, 7)
    first, second = jax.random.split(key)
    shape = (SECTIONS, 2, NROWS, COLS)
    level = jnp.arange(SECTIONS, dtype=jnp.float32) / (SECTIONS - 1)
    rise = jnp.power(jnp.float32(3.0), level)
    base = jax.random.truncated_normal(first, -3.0, 3.0, shape, jnp.float32)
    factor = jnp.exp(jax.random.uniform(second, shape, jnp.float32, -math.log(2.0), math.log(2.0)))
    return 0.2 * rise[:, None, None, None] * factor * base


def set_ends(values, rng, smallest, largest):
    longest = values.shape.index(max(values.shape))
    spots = []
    for shift in (0, 1):
        where = [jax.random.randint(jax.random.fold_in(rng, axis), (), 0, length) for axis, length in enumerate(values.shape)]
        where[longest] = (where[longest] + shift) % values.shape[longest]
        spots.append(tuple(where))
    return values.at[spots[0]].set(smallest).at[spots[1]].set(largest)


def levels(rng, extent, pieces, low, top_value):
    factor_of = 1.0
    for axis_at, parts in pieces:
        heights = jax.random.uniform(jax.random.fold_in(jax.random.fold_in(rng, 6), axis_at), (parts,), jnp.float32, low / len(pieces), top_value / len(pieces))
        factor_of = factor_of * jnp.repeat(jnp.exp(heights), extent[axis_at] // parts).reshape((-1,) + (1,) * (len(extent) - 1 - axis_at))
    return factor_of


def bell_draw(key, extent, width, most, shards=(), kind=jnp.bfloat16):
    loudness = levels(key, extent, shards, -0.22, 0.18) if shards else 1.0
    drawn = jax.random.normal(key, extent, jnp.float32) * width * loudness
    return jnp.minimum(jnp.maximum(drawn, -most), most).astype(kind)


def setup_inputs(seed: int = 0) -> dict:
    keys = jax.random.split(jax.random.key(seed), 8)
    return {
        "positions": bell_draw(keys[0], (SECTIONS, 2, NROWS, COLS), 0.5, 3.0, ((0, 64), (2, 8)), jnp.float32),
        "velocity": draw_velocity(jax.random.fold_in(keys[7], 71), 0),
        "flow_down": jnp.clip(1.0 * jax.random.uniform(keys[2], (SECTIONS, 2, NROWS, COLS), jnp.float32) ** levels(keys[2], (SECTIONS, 2, NROWS, COLS), ((0, 64), (2, 8)), -0.2, 0.2), 0.0, 1.0),
        "flow_up": jnp.clip(1.0 * jax.random.uniform(keys[3], (SECTIONS, 2, NROWS, COLS), jnp.float32) ** levels(keys[3], (SECTIONS, 2, NROWS, COLS), ((0, 64), (2, 8)), -0.2, 0.2), 0.0, 1.0),
        "flow_mask": set_ends((jax.random.randint(keys[4], (2, SECTIONS, NROWS, COLS), 0, 4) < 3).astype(jnp.int32), jax.random.fold_in(keys[4], 1), 0, 1),
        "resets": set_ends((jax.random.randint(keys[5], (STEPS, SECTIONS), 0, 3) < 1).astype(jnp.int32), jax.random.fold_in(keys[5], 1), 0, 1),
        "dt_index": jax.random.randint(keys[6], (STEPS,), 0, 5).astype(jnp.int32),
    }


def shift_left(field):
    return jnp.concatenate([field[..., 1:], jnp.zeros_like(field[..., :1])], axis=-1)

def shift_right(field):
    return jnp.concatenate([jnp.zeros_like(field[..., :1]), field[..., :-1]], axis=-1)

def bilinear(block, flow):
    top = block[:, :, 1:-1]
    lower = block[:, :, 2:]
    frac_row = flow[:, 0:1]
    frac_col = flow[:, 1:2]
    upper_mix = (1.0 - frac_col) * top + frac_col * shift_left(top)
    lower_mix = (1.0 - frac_col) * lower + frac_col * shift_left(lower)
    return (1.0 - frac_row) * upper_mix + frac_row * lower_mix

def spring_force(padded, flow_down, flow_up, down_valid, up_valid, row_ids, nrows):
    field = padded[1:-1, :, 1:-1]
    north = padded[1:-1, :, :-2]
    south = padded[1:-1, :, 2:]
    cols = field.shape[-1]
    in_north = (row_ids > 0).astype(jnp.float32)[:, None]
    in_south = (row_ids < nrows - 1).astype(jnp.float32)[:, None]
    col_ids = jnp.arange(cols)
    in_west = (col_ids > 0).astype(jnp.float32)
    in_east = (col_ids < cols - 1).astype(jnp.float32)
    intra = in_north * (north - field) + in_south * (south - field)
    intra = intra + in_west * (shift_right(field) - field) + in_east * (shift_left(field) - field)
    towards_prev = down_valid * (flow_down + bilinear(padded[:-2], flow_down) - field)
    towards_next = up_valid * (flow_up + bilinear(padded[2:], flow_up) - field)
    return 1.0 * intra + 1.0 * (towards_prev + towards_next)

def reference(positions, velocity, flow_down, flow_up, flow_mask, resets, dt_index):
    sections = positions.shape[0]
    nrows = positions.shape[2]
    sec_ids = jnp.arange(sections)
    row_ids = jnp.arange(nrows)
    down_valid = (flow_mask[0] * (sec_ids > 0).astype(jnp.int32)[:, None, None]).astype(jnp.float32)[:, None]
    up_valid = (flow_mask[1] * (sec_ids < sections - 1).astype(jnp.int32)[:, None, None]).astype(jnp.float32)[:, None]
    field = positions
    speed = velocity
    alpha = jnp.full((sections,), 0.1, jnp.float32)
    for step in range(STEPS):
        padded = jnp.pad(field, ((1, 1), (0, 0), (1, 1), (0, 0)))
        force = spring_force(padded, flow_down, flow_up, down_valid, up_valid, row_ids, nrows)
        dt = 0.1 * jnp.power(jnp.float32(1.25), dt_index[step].astype(jnp.float32))
        reset = resets[step] == 1
        alpha = jnp.where(reset, jnp.float32(0.1), 0.99 * alpha)
        factor = alpha[:, None, None, None]
        force_sq = jnp.sum(force * force)
        kicked = speed + dt * force
        kicked_sq = jnp.sum(kicked * kicked)
        mixed = (1.0 - factor) * kicked + factor * jnp.sqrt(kicked_sq / (force_sq + 1e-06)) * force
        speed = jnp.where(reset[:, None, None, None], jnp.zeros_like(mixed), mixed)
        field = field + dt * speed
    return (field, speed)
```

```python
import jax
import jax.numpy as jnp
from jax import lax
from jax.experimental import pallas as pl
from jax.experimental.pallas import tpu as pltpu
from jax.sharding import Mesh, PartitionSpec as P

GZ = ("z", "x")
X_CHIPS = 4
DEEP = 3
VMEM = pl.BlockSpec(memory_space=pltpu.VMEM)
SMEM = pl.BlockSpec(memory_space=pltpu.SMEM)
N_SUMS = 28


def exchange(value, axes, size):
    up = [(i, i + 1) for i in range(size - 1)]
    down = [(j, i) for i, j in up]
    return lax.ppermute(value, axes, up), lax.ppermute(value, axes, down)


class Stencil:
    def __init__(self, strip, nstrips, flow_down, flow_up, mask_down, mask_up):
        rows, cols = mask_down.shape
        own = rows - 8
        ring = lax.broadcasted_iota(jnp.int32, (rows, 1), 0)
        row = strip * own + jnp.where(ring < own + 4, ring, ring - rows)
        last = nstrips * own - 1
        self.north = jnp.where((row > 0) & (row <= last), 1.0, 0.0).astype(jnp.float32)
        self.south = jnp.where((row >= 0) & (row < last), 1.0, 0.0).astype(jnp.float32)
        col = lax.broadcasted_iota(jnp.int32, (1, cols), 1)
        self.west = jnp.where(col > 0, 1.0, 0.0).astype(jnp.float32)
        self.east = jnp.where(col < cols - 1, 1.0, 0.0).astype(jnp.float32)
        self.down = flow_down
        self.up = flow_up
        self.mask_down = mask_down
        self.mask_up = mask_up
        degree = (self.north + self.south) + (self.west + self.east)
        self.pull = degree + (mask_down + mask_up)
        self.rows, self.cols = rows, cols

    def below(self, value):
        return pltpu.roll(value, self.rows - 1, 0)

    def above(self, value):
        return pltpu.roll(value, 1, 0)

    def right(self, value):
        return pltpu.roll(value, self.cols - 1, 1) * self.east

    def left(self, value):
        return pltpu.roll(value, 1, 1) * self.west

    def sample(self, value, flow):
        step = self.right(value) - value
        here = value + flow[1] * step
        lower = self.below(value) + flow[1] * self.below(step)
        return here + flow[0] * (lower - here)

    def __call__(self, own, before, after):
        total = self.north * self.above(own) + self.south * self.below(own)
        total = total + (self.left(own) + self.right(own)) - self.pull * own
        total = total + self.mask_down * self.sample(before, self.down)
        return total + self.mask_up * self.sample(after, self.up)

    def bias(self, comp):
        return self.mask_down * self.down[comp] + self.mask_up * self.up[comp]


def stencil_of(ids, nstrips, fd, fu, mk):
    return Stencil(ids[0], nstrips, (fd[0], fd[1]), (fu[0], fu[1]), mk[0], mk[1])


def factors(reset, alpha):
    alpha = jnp.where(reset > 0.5, jnp.float32(0.1), 0.99 * alpha)
    keep = jnp.where(reset > 0.5, jnp.float32(0.0), jnp.float32(1.0))
    return alpha, (1.0 - alpha) * keep, alpha * keep


def resets_of(field):
    at = field.shape[1] - 5
    return field[0, at : at + 1], field[0, at + 1 : at + 2]


def after_first(u0, v0, f0, dt0, k0, g0):
    va = k0 * (v0 + dt0 * f0)
    vb = g0 * f0
    return va, vb, u0 + dt0 * va, dt0 * vb


def after_second(first, fa, fb, dt1, k1, g1):
    va, vb, ua, ub = first
    vel = (k1 * (va + dt1 * fa), k1 * (vb + dt1 * fb), g1 * fa, g1 * fb)
    return vel, (ua + dt1 * vel[0], ub + dt1 * vel[1], dt1 * vel[2], dt1 * vel[3])


def first_kernel(nstrips, ids, u, ub, ua, v, fd, fu, mk, out):
    op = stencil_of(ids, nstrips, fd, fu, mk)
    for c in range(2):
        out[c] = op(u[c], ub[c], ua[c]) + op.bias(c)
        out[2 + c] = v[c]


def second_kernel(nstrips, ids, dts, u, ub, ua, p, pb, pa, fd, fu, mk, out):
    op = stencil_of(ids, nstrips, fd, fu, mk)
    weights = [factors(resets_of(f)[0], jnp.float32(0.1)) for f in (u, ub, ua)]
    for c in range(2):
        parts = [
            after_first(f[c], q[2 + c], q[c], dts[0], k, g)
            for f, q, (_, k, g) in zip((u, ub, ua), (p, pb, pa), weights)
        ]
        out[c] = op(*[x[2] for x in parts]) + op.bias(c)
        out[2 + c] = op(*[x[3] for x in parts])


def products(fields):
    return [fields[i] * fields[j] for i in range(len(fields)) for j in range(i, len(fields))]


def tile_sum(value):
    rows = value.shape[0]
    tall = value[0:8]
    for r in range(8, rows, 8):
        tall = tall + value[r : r + 8]
    total = tall[:, 0:128]
    for col in range(128, value.shape[1], 128):
        total = total + tall[:, col : col + 128]
    return total


def third_kernel(nstrips, ids, dts, u, ub, ua, p, pb, pa, q, qb, qa, fd, fu, mk, out, sums):
    op = stencil_of(ids, nstrips, fd, fu, mk)
    rows = out.shape[1]
    dt0, dt1, dt2 = dts[0], dts[1], dts[2]
    weights = []
    for f in (u, ub, ua):
        r0, r1 = resets_of(f)
        alpha, k0, g0 = factors(r0, jnp.float32(0.1))
        _, k1, g1 = factors(r1, alpha)
        weights.append((k0, g0, k1, g1))
    totals = [None] * N_SUMS
    for c in range(2):
        sides = []
        for f, m, n, (k0, g0, k1, g1) in zip((u, ub, ua), (p, pb, pa), (q, qb, qa), weights):
            one = after_first(f[c], m[2 + c], m[c], dt0, k0, g0)
            sides.append((one, *after_second(one, n[c], n[2 + c], dt1, k1, g1)))
        forces = []
        for i in range(4):
            force = op(sides[0][2][i], sides[1][2][i], sides[2][2][i])
            if i == 0:
                force = force + op.bias(c)
            force = force[:rows]
            out[4 * c + i] = force
            forces.append(force)
        va, vb = sides[0][0][0][:rows], sides[0][0][1][:rows]
        f0, fa, fb = p[c, :rows], q[c, :rows], q[2 + c, :rows]
        kicked = [x[:rows] + dt2 * y for x, y in zip(sides[0][1], forces)]
        terms = products([f0]) + products([p[2 + c, :rows] + dt0 * f0])
        terms += products([fa, fb]) + products([va + dt1 * fa, vb + dt1 * fb])
        terms += products(forces) + products(kicked)
        for i, term in enumerate(terms):
            part = tile_sum(term)
            totals[i] = part if c == 0 else totals[i] + part
    lane = lax.broadcasted_iota(jnp.int32, (1, 128), 1)
    row = jnp.zeros((1, 128), jnp.float32)
    for i, total in enumerate(totals):
        whole = jnp.sum(jnp.sum(total, axis=0, keepdims=True), axis=1, keepdims=True)
        row = jnp.where(lane == i, whole, row)
    sums[...] = row


def form(sums, at, size, basis):
    total = None
    for i in range(size):
        for j in range(i, size):
            term = sums[:, at : at + 1]
            at += 1
            for b in basis[i] + basis[j]:
                term = term * b
            if i != j:
                term = 2.0 * term
            total = term if total is None else total + term
    return jnp.maximum(total, 0.0)


def ratio(kicked, force):
    return jnp.sqrt(kicked / (force + 1e-06))


def last_kernel(dts, rs, parts, u, p, q, f2, pos, vel):
    rows = pos.shape[1]
    sums = jnp.sum(parts[...], axis=0)
    c0 = ratio(jnp.maximum(sums[:, 1:2], 0.0), sums[:, 0:1])
    one = ((), (c0,))
    c1 = ratio(form(sums, 5, 2, one), form(sums, 2, 2, one))
    two = ((), (c0,), (c1,), (c0, c1))
    c2 = ratio(form(sums, 18, 4, two), form(sums, 8, 4, two))
    alpha = jnp.float32(0.1)
    weights = []
    for i in range(3):
        alpha = jnp.where(rs[i] == 1, jnp.float32(0.1), 0.99 * alpha)
        keep = jnp.where(rs[i] == 1, jnp.float32(0.0), jnp.float32(1.0))
        weights.append(((1.0 - alpha) * keep, alpha * keep))
    for c in range(2):
        f = f2[4 * c] + c0 * f2[4 * c + 1] + c1 * (f2[4 * c + 2] + c0 * f2[4 * c + 3])
        field, speed = u[c, :rows], p[2 + c, :rows]
        forces = (p[c, :rows], q[c, :rows] + c0 * q[2 + c, :rows], f)
        for i, (force, factor) in enumerate(zip(forces, (c0, c1, c2))):
            keep, mix = weights[i]
            speed = keep * (speed + dts[i] * force) + (mix * factor) * force
            field = field + dts[i] * speed
        pos[c] = field
        vel[c] = speed


def call(kernel, out_shape, specs, *args):
    return pl.pallas_call(
        kernel,
        out_shape=out_shape,
        in_specs=specs,
        out_specs=jax.tree.map(lambda _: VMEM, out_shape),
        compiler_params=pltpu.CompilerParams(vmem_limit_bytes=40 * 2**20),
    )(*args)


def f32(*shape):
    return jax.ShapeDtypeStruct(shape, jnp.float32)


def local(positions, velocity, flow_down, flow_up, flow_mask, resets, dt_index):
    nstrips, nz, nx = lax.axis_size("strip"), lax.axis_size("z"), lax.axis_size("x")
    section = lax.axis_index(GZ)
    _, comps, rows, cols = positions.shape
    ring = rows + 8
    valid = jnp.stack([section > 0, section < nz * nx - 1]).astype(jnp.int32)
    masks = (flow_mask[:, 0] * valid[:, None, None]).astype(jnp.float32)
    dts = 0.1 * jnp.power(jnp.float32(1.25), dt_index.astype(jnp.float32))
    ids = jnp.reshape(lax.axis_index("strip"), (1,))
    resets = resets[:, 0]
    fields = [positions[0], velocity[0], flow_down[0], flow_up[0], masks]
    deep = [DEEP] + [DEEP - 1] * 4

    def packed(cut):
        slabs = [cut(f, d).reshape(-1, cols) for f, d in zip(fields, deep)]
        return jnp.concatenate(slabs + [jnp.zeros((2, cols), jnp.float32)], axis=0)

    from_above = packed(lambda f, d: f[:, rows - d :])
    from_below = packed(lambda f, d: f[:, :d])
    above = lax.ppermute(from_above, "strip", [(i, i + 1) for i in range(nstrips - 1)])
    below = lax.ppermute(from_below, "strip", [(i + 1, i) for i in range(nstrips - 1)])
    marks = (resets[:2] == 1).astype(jnp.float32)
    wide, at = [], 0
    for f, d in zip(fields, deep):
        lower = below[at : at + 2 * d].reshape(2, d, cols)
        upper = above[at : at + 2 * d].reshape(2, d, cols)
        at += 2 * d
        if d == DEEP:
            gap = jnp.broadcast_to(marks[None, :, None], (2, 2, cols))
        else:
            gap = jnp.zeros((2, 8 - 2 * d, cols), jnp.float32)
        wide.append(jnp.concatenate([f, lower, gap, upper], axis=1))
    u, v, fd, fu, mk = wide

    ub, ua = exchange(u, GZ, nz * nx)
    p = call(
        lambda *refs: first_kernel(nstrips, *refs),
        f32(4, ring, cols),
        [SMEM] + [VMEM] * 7,
        ids, u, ub, ua, v, fd, fu, mk,
    )
    pb, pa = exchange(p, GZ, nz * nx)
    q = call(
        lambda *refs: second_kernel(nstrips, *refs),
        f32(4, ring, cols),
        [SMEM] * 2 + [VMEM] * 9,
        ids, dts, u, ub, ua, p, pb, pa, fd, fu, mk,
    )
    qb, qa = exchange(q, GZ, nz * nx)
    f2, sums = call(
        lambda *refs: third_kernel(nstrips, *refs),
        (f32(8, rows, cols), f32(1, 128)),
        [SMEM] * 2 + [VMEM] * 12,
        ids, dts, u, ub, ua, p, pb, pa, q, qb, qa, fd, fu, mk,
    )
    near = nx * nstrips
    sums = lax.all_to_all(jnp.broadcast_to(sums, (near, 1, 128)), ("x", "strip"), 0, 0)
    sums = jnp.sum(sums, axis=0)
    sums = lax.all_to_all(jnp.broadcast_to(sums, (nz, 1, 128)), "z", 0, 0)
    pos, vel = call(
        last_kernel,
        (f32(comps, rows, cols), f32(comps, rows, cols)),
        [SMEM] * 2 + [VMEM] * 5,
        dts, resets, sums, u, p, q, f2,
    )
    return pos[None], vel[None]


def solution(mesh):
    sections, strips = mesh.devices.shape
    split = mesh.devices.reshape(sections // X_CHIPS, X_CHIPS, strips)
    field = P(GZ, None, "strip", None)
    placed = (field, field, field, field, P(None, GZ, "strip", None), P(None, GZ), P())
    return jax.shard_map(
        local,
        mesh=Mesh(split, ("z", "x", "strip")),
        in_specs=placed,
        out_specs=(field, field),
        check_vma=False,
    )
```

```python
import jax
import jax.numpy as jnp
from jax import lax
from jax.experimental import pallas as pl
from jax.experimental.pallas import tpu as pltpu
from jax.sharding import Mesh, PartitionSpec as P

GZ = ("z", "x")
X_CHIPS = 4
DEEP = 3
VMEM = pl.BlockSpec(memory_space=pltpu.VMEM)
SMEM = pl.BlockSpec(memory_space=pltpu.SMEM)
N_SUMS = 28


def swap(value, size):
    first = [(i, i ^ 1) for i in range(size)]
    second = [(i, ((i - 1) ^ 1) + 1) for i in range(1, size - 1)]
    return lax.ppermute(value, GZ, first), lax.ppermute(value, GZ, second)


class Stencil:
    def __init__(self, strip, nstrips, flow_down, flow_up, mask_down, mask_up):
        rows, cols = mask_down.shape
        own = rows - 8
        ring = lax.broadcasted_iota(jnp.int32, (rows, 1), 0)
        row = strip * own + jnp.where(ring < own + 4, ring, ring - rows)
        last = nstrips * own - 1
        self.north = jnp.where((row > 0) & (row <= last), 1.0, 0.0).astype(jnp.float32)
        self.south = jnp.where((row >= 0) & (row < last), 1.0, 0.0).astype(jnp.float32)
        col = lax.broadcasted_iota(jnp.int32, (1, cols), 1)
        self.west = jnp.where(col > 0, 1.0, 0.0).astype(jnp.float32)
        self.east = jnp.where(col < cols - 1, 1.0, 0.0).astype(jnp.float32)
        self.down = flow_down
        self.up = flow_up
        self.mask_down = mask_down
        self.mask_up = mask_up
        degree = (self.north + self.south) + (self.west + self.east)
        self.pull = degree + (mask_down + mask_up)
        self.rows, self.cols = rows, cols

    def below(self, value):
        return pltpu.roll(value, self.rows - 1, 0)

    def above(self, value):
        return pltpu.roll(value, 1, 0)

    def right(self, value):
        return pltpu.roll(value, self.cols - 1, 1) * self.east

    def left(self, value):
        return pltpu.roll(value, 1, 1) * self.west

    def sample(self, value, flow):
        step = self.right(value) - value
        here = value + flow[1] * step
        lower = self.below(value) + flow[1] * self.below(step)
        return here + flow[0] * (lower - here)

    def __call__(self, own, before, after):
        total = self.north * self.above(own) + self.south * self.below(own)
        total = total + (self.left(own) + self.right(own)) - self.pull * own
        total = total + self.mask_down * self.sample(before, self.down)
        return total + self.mask_up * self.sample(after, self.up)

    def bias(self, comp):
        return self.mask_down * self.down[comp] + self.mask_up * self.up[comp]


def stencil_of(ids, nstrips, fd, fu, mk):
    return Stencil(ids[0], nstrips, (fd[0], fd[1]), (fu[0], fu[1]), mk[0], mk[1])


def factors(reset, alpha):
    alpha = jnp.where(reset > 0.5, jnp.float32(0.1), 0.99 * alpha)
    keep = jnp.where(reset > 0.5, jnp.float32(0.0), jnp.float32(1.0))
    return alpha, (1.0 - alpha) * keep, alpha * keep


def from_neighbour(packet, rows, at):
    tail = packet[4 * rows :]
    tail = tail if at == 0 else pltpu.roll(tail, 8 - at, 0)
    return jnp.concatenate([packet[rows * at : rows * at + rows], tail], axis=0)


def weights_of(marks):
    weights = []
    for side in range(3):
        alpha, keep, mix = factors(marks[3 * side], jnp.float32(0.1))
        weights.append((keep, mix, *factors(marks[3 * side + 1], alpha)[1:]))
    return weights


def after_first(u0, v0, f0, dt0, k0, g0):
    va = k0 * (v0 + dt0 * f0)
    vb = g0 * f0
    return va, vb, u0 + dt0 * va, dt0 * vb


def after_second(first, fa, fb, dt1, k1, g1):
    va, vb, ua, ub = first
    vel = (k1 * (va + dt1 * fa), k1 * (vb + dt1 * fb), g1 * fa, g1 * fb)
    return vel, (ua + dt1 * vel[0], ub + dt1 * vel[1], dt1 * vel[2], dt1 * vel[3])


def first_kernel(nstrips, ids, u, ue, uo, fe, fo, mk, out):
    op = stencil_of(ids, nstrips, fe, fo, mk)
    for c in range(2):
        out[c] = op(u[c], ue[c], uo[c]) + op.bias(c)


def second_kernel(nstrips, ids, dts, marks, u, ue, uo, v, ve, vo, p, pe, po, fe, fo, mk, q, tails):
    op = stencil_of(ids, nstrips, fe, fo, mk)
    rows = p.shape[1] - 8
    q[4 * rows :] = jnp.zeros((8, q.shape[1]), jnp.float32)
    for c in range(2):
        parts = [
            after_first(f[c], w[c], x[c], dts[0], k[0], k[1])
            for f, w, x, k in zip((u, ue, uo), (v, ve, vo), (p, pe, po), weights_of(marks))
        ]
        for i in range(2):
            force = op(*[x[2 + i] for x in parts])
            if i == 0:
                force = force + op.bias(c)
            at = 2 * i + c
            q[rows * at : rows * at + rows] = force[:rows]
            q[4 * rows + at : 4 * rows + at + 1] = force[rows : rows + 1]
            tails[8 * at : 8 * at + 8] = force[rows:]


def products(fields):
    return [fields[i] * fields[j] for i in range(len(fields)) for j in range(i, len(fields))]


def tile_sum(value):
    rows = value.shape[0]
    tall = value[0:8]
    for r in range(8, rows, 8):
        tall = tall + value[r : r + 8]
    total = tall[:, 0:128]
    for col in range(128, value.shape[1], 128):
        total = total + tall[:, col : col + 128]
    return total


def third_kernel(nstrips, ids, dts, marks, u, ue, uo, v, ve, vo, p, pe, po, q, tails, qe, qo, fe, fo, mk, out, sums):
    op = stencil_of(ids, nstrips, fe, fo, mk)
    rows = out.shape[1]
    dt0, dt1, dt2 = dts[0], dts[1], dts[2]
    weights = weights_of(marks)
    totals = [None] * N_SUMS
    for c in range(2):
        cores = [q[rows * at : rows * at + rows] for at in (c, 2 + c)]
        own = [
            jnp.concatenate([core, tails[8 * at : 8 * at + 8]], axis=0)
            for core, at in zip(cores, (c, 2 + c))
        ]
        even = [from_neighbour(qe, rows, at) for at in (c, 2 + c)]
        odd = [from_neighbour(qo, rows, at) for at in (c, 2 + c)]
        sides = []
        for f, w, x, n, (k0, g0, k1, g1) in zip((u, ue, uo), (v, ve, vo), (p, pe, po), (own, even, odd), weights):
            one = after_first(f[c], w[c], x[c], dt0, k0, g0)
            sides.append((one, *after_second(one, n[0], n[1], dt1, k1, g1)))
        forces = []
        for i in range(4):
            force = op(sides[0][2][i], sides[1][2][i], sides[2][2][i])
            if i == 0:
                force = force + op.bias(c)
            force = force[:rows]
            out[4 * c + i] = force
            forces.append(force)
        va, vb = sides[0][0][0][:rows], sides[0][0][1][:rows]
        f0, (fa, fb) = p[c, :rows], cores
        kicked = [x[:rows] + dt2 * y for x, y in zip(sides[0][1], forces)]
        terms = products([f0]) + products([v[c, :rows] + dt0 * f0])
        terms += products([fa, fb]) + products([va + dt1 * fa, vb + dt1 * fb])
        terms += products(forces) + products(kicked)
        for i, term in enumerate(terms):
            part = tile_sum(term)
            totals[i] = part if c == 0 else totals[i] + part
    lane = lax.broadcasted_iota(jnp.int32, (1, 128), 1)
    row = jnp.zeros((1, 128), jnp.float32)
    for i, total in enumerate(totals):
        whole = jnp.sum(jnp.sum(total, axis=0, keepdims=True), axis=1, keepdims=True)
        row = jnp.where(lane == i, whole, row)
    sums[...] = row


def form(sums, at, size, basis):
    total = None
    for i in range(size):
        for j in range(i, size):
            term = sums[:, at : at + 1]
            at += 1
            for b in basis[i] + basis[j]:
                term = term * b
            if i != j:
                term = 2.0 * term
            total = term if total is None else total + term
    return jnp.maximum(total, 0.0)


def ratio(kicked, force):
    return jnp.sqrt(kicked / (force + 1e-06))


def last_kernel(dts, marks, parts, u, v, p, q, f2, pos, vel):
    rows = pos.shape[1]
    sums = jnp.sum(parts[...], axis=0)
    c0 = ratio(jnp.maximum(sums[:, 1:2], 0.0), sums[:, 0:1])
    one = ((), (c0,))
    c1 = ratio(form(sums, 5, 2, one), form(sums, 2, 2, one))
    two = ((), (c0,), (c1,), (c0, c1))
    c2 = ratio(form(sums, 18, 4, two), form(sums, 8, 4, two))
    alpha = jnp.float32(0.1)
    weights = []
    for i in range(3):
        alpha, keep, mix = factors(marks[i], alpha)
        weights.append((keep, mix))
    for c in range(2):
        f = f2[4 * c] + c0 * f2[4 * c + 1] + c1 * (f2[4 * c + 2] + c0 * f2[4 * c + 3])
        field, speed = u[c, :rows], v[c, :rows]
        cores = [q[rows * at : rows * at + rows] for at in (c, 2 + c)]
        forces = (p[c, :rows], cores[0] + c0 * cores[1], f)
        for i, (force, factor) in enumerate(zip(forces, (c0, c1, c2))):
            keep, mix = weights[i]
            speed = keep * (speed + dts[i] * force) + (mix * factor) * force
            field = field + dts[i] * speed
        pos[c] = field
        vel[c] = speed


def call(kernel, out_shape, specs, *args):
    return pl.pallas_call(
        kernel,
        out_shape=out_shape,
        in_specs=specs,
        out_specs=jax.tree.map(lambda _: VMEM, out_shape),
        compiler_params=pltpu.CompilerParams(vmem_limit_bytes=40 * 2**20),
    )(*args)


def f32(*shape):
    return jax.ShapeDtypeStruct(shape, jnp.float32)


def local(positions, velocity, flow_down, flow_up, flow_mask, resets, dt_index):
    nstrips, nz, nx = lax.axis_size("strip"), lax.axis_size("z"), lax.axis_size("x")
    section = lax.axis_index(GZ)
    _, comps, rows, cols = positions.shape
    ring = rows + 8
    core = f32(comps, rows, cols)
    marks = (resets[:, 0] == 1).astype(jnp.float32)
    tile = jnp.broadcast_to(jnp.pad(marks, (0, 5))[:, None], (8, cols))
    start = [positions.reshape(-1, cols), velocity.reshape(-1, cols), tile]
    even, odd = swap(jnp.concatenate(start, axis=0), nz * nx)
    ends = [(x[: 2 * rows].reshape(2, rows, cols), x[2 * rows : 4 * rows].reshape(2, rows, cols)) for x in (even, odd)]
    marks = jnp.concatenate([marks] + [x[4 * rows : 4 * rows + 3, 0] for x in (even, odd)])
    dts = 0.1 * jnp.power(jnp.float32(1.25), dt_index.astype(jnp.float32))
    ids = jnp.reshape(lax.axis_index("strip"), (1,))
    is_odd = section % 2 == 1
    valid = jnp.stack([section > 0, section < nz * nx - 1]).astype(jnp.int32)
    masks = (flow_mask[:, 0] * valid[:, None, None]).astype(jnp.float32)
    masks = jnp.where(is_odd, masks, masks[::-1])
    flow_even = jnp.where(is_odd, flow_down[0], flow_up[0])
    flow_odd = jnp.where(is_odd, flow_up[0], flow_down[0])
    fields = [positions[0], velocity[0], flow_even, flow_odd, masks, *ends[0], *ends[1]]
    deep = [DEEP] + [DEEP - 1] * 4 + [DEEP, DEEP - 1] * 2
    spare = jnp.zeros((-2 * sum(deep) % 8, cols), jnp.float32)

    def packed(cut):
        slabs = [cut(f, d).reshape(-1, cols) for f, d in zip(fields, deep)]
        return jnp.concatenate(slabs + [spare], axis=0)

    from_above = packed(lambda f, d: f[:, rows - d :])
    from_below = packed(lambda f, d: f[:, :d])
    above = lax.ppermute(from_above, "strip", [(i, i + 1) for i in range(nstrips - 1)])
    below = lax.ppermute(from_below, "strip", [(i + 1, i) for i in range(nstrips - 1)])
    wide, at = [], 0
    for f, d in zip(fields, deep):
        lower = below[at : at + 2 * d].reshape(2, d, cols)
        upper = above[at : at + 2 * d].reshape(2, d, cols)
        at += 2 * d
        gap = jnp.zeros((2, 8 - 2 * d, cols), jnp.float32)
        wide.append(jnp.concatenate([f, lower, gap, upper], axis=1))
    u, v, fe, fo, mk, ue, ve, uo, vo = wide

    p = call(
        lambda *refs: first_kernel(nstrips, *refs),
        f32(comps, ring, cols),
        [SMEM] + [VMEM] * 6,
        ids, u, ue, uo, fe, fo, mk,
    )
    pe, po = swap(p, nz * nx)
    q, tails = call(
        lambda *refs: second_kernel(nstrips, *refs),
        (f32(4 * rows + 8, cols), f32(32, cols)),
        [SMEM] * 3 + [VMEM] * 12,
        ids, dts, marks, u, ue, uo, v, ve, vo, p, pe, po, fe, fo, mk,
    )
    qe, qo = swap(q, nz * nx)
    f2, sums = call(
        lambda *refs: third_kernel(nstrips, *refs),
        (f32(4 * comps, rows, cols), f32(1, 128)),
        [SMEM] * 3 + [VMEM] * 16,
        ids, dts, marks, u, ue, uo, v, ve, vo, p, pe, po, q, tails, qe, qo, fe, fo, mk,
    )
    near = nx * nstrips
    sums = lax.all_to_all(jnp.broadcast_to(sums, (near, 1, 128)), ("x", "strip"), 0, 0)
    sums = jnp.sum(sums, axis=0)
    sums = lax.all_to_all(jnp.broadcast_to(sums, (nz, 1, 128)), "z", 0, 0)
    pos, vel = call(
        last_kernel,
        (core, core),
        [SMEM] * 2 + [VMEM] * 6,
        dts, marks, sums, u, v, p, q, f2,
    )
    return pos[None], vel[None]


def solution(mesh):
    sections, strips = mesh.devices.shape
    split = mesh.devices.reshape(sections // X_CHIPS, X_CHIPS, strips)
    field = P(GZ, None, "strip", None)
    placed = (field, field, field, field, P(None, GZ, "strip", None), P(None, GZ), P())
    return jax.shard_map(
        local,
        mesh=Mesh(split, ("z", "x", "strip")),
        in_specs=placed,
        out_specs=(field, field),
        check_vma=False,
    )
```

```python
import jax
import jax.numpy as jnp
from jax import lax
from jax.experimental import pallas as pl
from jax.experimental.pallas import tpu as pltpu
from jax.sharding import Mesh, PartitionSpec as P

GZ = ("z", "x")
X_CHIPS = 4
DEEP = (3, 2, 2, 2, 2, 3, 2, 3, 2)
VMEM = pl.BlockSpec(memory_space=pltpu.VMEM)
SMEM = pl.BlockSpec(memory_space=pltpu.SMEM)
ANY = pl.BlockSpec(memory_space=pl.ANY)


def swap(value, axes, size):
    first = [(i, i ^ 1) for i in range(size)]
    second = [(i, ((i - 1) ^ 1) + 1) for i in range(1, size - 1)]
    values = value if isinstance(value, tuple) else (value, value)
    return lax.ppermute(values[0], axes, first), lax.ppermute(values[1], axes, second)


class Stencil:
    def __init__(self, strip, nstrips, flow_even, flow_odd, mask_even, mask_odd):
        rows, cols = mask_even.shape
        own = rows - 8
        ring = lax.broadcasted_iota(jnp.int32, (rows, 1), 0)
        row = strip * own + jnp.where(ring < own + 4, ring, ring - rows)
        last = nstrips * own - 1
        self.north = jnp.where((row > 0) & (row <= last), 1.0, 0.0).astype(jnp.float32)
        self.south = jnp.where((row >= 0) & (row < last), 1.0, 0.0).astype(jnp.float32)
        col = lax.broadcasted_iota(jnp.int32, (1, cols), 1)
        self.west = jnp.where(col > 0, 1.0, 0.0).astype(jnp.float32)
        self.east = jnp.where(col < cols - 1, 1.0, 0.0).astype(jnp.float32)
        self.flow_even = flow_even
        self.flow_odd = flow_odd
        self.mask_even = mask_even
        self.mask_odd = mask_odd
        degree = (self.north + self.south) + (self.west + self.east)
        self.pull = degree + (mask_even + mask_odd)
        self.rows, self.cols = rows, cols

    def below(self, value):
        return pltpu.roll(value, self.rows - 1, 0)

    def above(self, value):
        return pltpu.roll(value, 1, 0)

    def right(self, value):
        return pltpu.roll(value, self.cols - 1, 1) * self.east

    def left(self, value):
        return pltpu.roll(value, 1, 1) * self.west

    def sample(self, value, flow):
        step = self.right(value) - value
        here = value + flow[1] * step
        lower = self.below(value) + flow[1] * self.below(step)
        return here + flow[0] * (lower - here)

    def inner(self, own):
        total = self.north * self.above(own) + self.south * self.below(own)
        return total + (self.left(own) + self.right(own)) - self.pull * own

    def even(self, value):
        return self.mask_even * self.sample(value, self.flow_even)

    def odd(self, value):
        return self.mask_odd * self.sample(value, self.flow_odd)

    def __call__(self, own, even, odd):
        return self.inner(own) + (self.even(even) + self.odd(odd))

    def bias(self, comp):
        return self.mask_even * self.flow_even[comp] + self.mask_odd * self.flow_odd[comp]


def stencil_of(ids, nstrips, fe, fo, mk):
    return Stencil(ids[0], nstrips, (fe[0], fe[1]), (fo[0], fo[1]), mk[0], mk[1])


def factors(reset, alpha):
    alpha = jnp.where(reset > 0.5, jnp.float32(0.1), 0.99 * alpha)
    keep = jnp.where(reset > 0.5, jnp.float32(0.0), jnp.float32(1.0))
    return alpha, (1.0 - alpha) * keep, alpha * keep


def gamma():
    return 0.99 * jnp.float32(0.1)


def weights_of(marks):
    weights = []
    for side in range(3):
        alpha = factors(marks[3 * side], jnp.float32(0.1))[0]
        rho = jnp.where(marks[3 * side] > 0.5, jnp.float32(0.0), jnp.float32(1.0))
        weights.append((rho, *factors(marks[3 * side + 1], alpha)[1:]))
    return weights


def start_kernel(pos, vel, tile, out, sems):
    rows = pos.shape[0]
    copies = [
        pltpu.make_async_copy(src, out.at[pl.ds(at, size)], sems.at[i])
        for i, (src, at, size) in enumerate(((pos, 0, rows), (vel, rows, rows), (tile, 2 * rows, 8)))
    ]
    for copy in copies:
        copy.start()
    for copy in copies:
        copy.wait()


def rims_kernel(ids, u, v, fe, fo, mk, even, odd, first, second):
    rows = u.shape[1]
    sides = [(x, rows * at) for x in (even, odd) for at in range(4)]
    comps = [(f.at[c], 0) for f in (u, v, fe, fo, mk) for c in range(2)]
    comps += [(x, at) for x, at in sides]

    def fill(upper, lower):
        at = 0
        for i, (src, base) in enumerate(comps):
            deep = DEEP[i // 2]
            upper[at : at + deep] = src[base : base + deep]
            lower[at : at + deep] = src[base + rows - deep : base + rows]
            at += deep
        for out in (upper, lower):
            out[at:] = jnp.zeros((out.shape[0] - at, out.shape[1]), jnp.float32)

    @pl.when(ids[0] % 2 == 1)
    def _():
        fill(first, second)

    @pl.when(ids[0] % 2 == 0)
    def _():
        fill(second, first)


def first_kernel(nstrips, ids, marks, u, ue, uo, v, ve, vo, fe, fo, mk, packet, tails):
    op = stencil_of(ids, nstrips, fe, fo, mk)
    rows = u.shape[1] - 8
    rho, rho_even, rho_odd = [w[0] for w in weights_of(marks)]
    end = 4 * rows
    for c in range(2):
        f0 = op(u[c], ue[c], uo[c]) + op.bias(c)
        h = op(rho * v[c], rho_even * ve[c], rho_odd * vo[c])
        for at, value in ((c, f0), (2 + c, h)):
            packet[rows * at : rows * at + rows] = value[:rows]
            tails[8 * at : 8 * at + 8] = value[rows:]
        packet[end + 3 * c : end + 3 * c + 2] = f0[rows : rows + 2]
        last = end + (7, 2)[c]
        packet[last : last + 1] = f0[rows + 7 :]
        packet[end + 5 + c : end + 6 + c] = h[rows : rows + 1]


def own_ring(packet, tails, rows, at):
    return jnp.concatenate([packet[rows * at : rows * at + rows], tails[8 * at : 8 * at + 8]], axis=0)


def side_ring(packet, rows, at, size, shift):
    tail = packet[size * rows :]
    tail = pltpu.roll(tail, 8 - shift, 0) if shift else tail
    return jnp.concatenate([packet[rows * at : rows * at + rows], tail], axis=0)


def side_force(packet, rows, c):
    return side_ring(packet, rows, c, 4, 3 * c)


def side_h(packet, rows, c):
    return side_ring(packet, rows, 2 + c, 4, 5 + c)


def second_kernel(nstrips, ids, marks, p, ptails, pe, po, fe, fo, mk, packet, tails):
    op = stencil_of(ids, nstrips, fe, fo, mk)
    rows = mk.shape[1] - 8
    rho, rho_even, rho_odd = [w[0] for w in weights_of(marks)]
    packet[2 * rows :] = jnp.zeros((8, packet.shape[1]), jnp.float32)
    for c in range(2):
        f0 = own_ring(p, ptails, rows, c)
        g = op(rho * f0, rho_even * side_force(pe, rows, c), rho_odd * side_force(po, rows, c))
        packet[rows * c : rows * c + rows] = g[:rows]
        packet[2 * rows + c : 2 * rows + c + 1] = g[rows : rows + 1]
        tails[8 * c : 8 * c + 8] = g[rows:]


def products(fields, pairs):
    return [fields[i] * fields[j] for i, j in pairs]


def all_pairs(size):
    return [(i, j) for i in range(size) for j in range(i, size)]


EARLY = [(0, 0), (0, 2), (2, 2)]
LATE = [pair for pair in all_pairs(4) if pair not in EARLY]
N_EARLY = 2 + 3 + 3 + 2 * len(EARLY)
N_LATE = 2 * len(LATE)


def tile_sum(value):
    rows = value.shape[0]
    tall = value[0:8]
    for r in range(8, rows, 8):
        tall = tall + value[r : r + 8]
    total = tall[:, 0:128]
    for col in range(128, value.shape[1], 128):
        total = total + tall[:, col : col + 128]
    return total


def lanes_of(totals, at):
    lane = lax.broadcasted_iota(jnp.int32, (1, 128), 1)
    row = jnp.zeros((1, 128), jnp.float32)
    for i, total in enumerate(totals):
        whole = jnp.sum(jnp.sum(total, axis=0, keepdims=True), axis=1, keepdims=True)
        row = jnp.where(lane == at + i, whole, row)
    return row


def gathered(totals, terms):
    parts = [tile_sum(term) for term in terms]
    return parts if totals is None else [x + y for x, y in zip(totals, parts)]


def third_kernel(nstrips, ids, dts, marks, v, ve, vo, p, ptails, pe, po, g, gtails, fe, fo, mk, f2, w2, sums):
    op = stencil_of(ids, nstrips, fe, fo, mk)
    rows = mk.shape[1] - 8
    dt0, dt1, dt2 = dts[0], dts[1], dts[2]
    kappa = 1.0 - gamma()
    weights = weights_of(marks)
    totals = None
    for c in range(2):
        f0s = [own_ring(p, ptails, rows, c), side_force(pe, rows, c), side_force(po, rows, c)]
        hs = [own_ring(p, ptails, rows, 2 + c), side_h(pe, rows, c), side_h(po, rows, c)]
        vs = [v[c], ve[c], vo[c]]
        ts = [f0 + (dt0 * kappa) * h for f0, h in zip(f0s, hs)]
        g0 = dt0 * own_ring(g, gtails, rows, c)
        one = [k1 * ((rho * kappa) * v0 + dt1 * t) for v0, t, (rho, k1, _) in zip(vs, ts, weights)]
        mix = [g1 * t for t, (_, _, g1) in zip(ts, weights)]
        rho, k1, g1 = weights[0]
        mu = k1 * (rho * f0s[0] + dt1 * g0)
        both = g1 * g0
        sides = [(w[1] * w[0]) * f0 for f0, w in zip(f0s[1:], weights[1:])]
        forces = [
            ts[0] + dt1 * op(*one),
            g0 + dt1 * op(mu, *sides),
            dt1 * op(*mix),
            dt1 * op.inner(both),
        ]
        forces = [f[:rows] for f in forces]
        kicked = [x[:rows] + dt2 * f for x, f in zip((one[0], mu, mix[0], both), forces)]
        for i in range(4):
            f2[4 * c + i] = forces[i]
            w2[4 * c + i] = kicked[i]
        f0, v0, t, g0 = f0s[0][:rows], vs[0][:rows], ts[0][:rows], g0[:rows]
        terms = products([f0, v0 + dt0 * f0], [(0, 0), (1, 1)]) + products([t, g0], all_pairs(2))
        terms += products([(rho * kappa) * v0 + dt1 * t, rho * f0 + dt1 * g0], all_pairs(2))
        terms += products(forces, EARLY) + products(kicked, EARLY)
        totals = gathered(totals, terms)
    sums[...] = lanes_of(totals, 0)


def fourth_kernel(nstrips, ids, dts, marks, part, w2, early, ge, go, fe, fo, mk, f2, sums):
    op = stencil_of(ids, nstrips, fe, fo, mk)
    rows = part.shape[1]
    dt0, dt1, dt2 = dts[0], dts[1], dts[2]
    weights = weights_of(marks)
    totals = None
    for c in range(2):
        even = op.even(side_ring(ge, rows, c, 2, c))[:rows]
        odd = op.odd(side_ring(go, rows, c, 2, c))[:rows]
        scale = dt1 * dt0
        mu = scale * dt1 * (weights[1][1] * even + weights[2][1] * odd)
        both = scale * (weights[1][2] * even + weights[2][2] * odd)
        forces = [part[4 * c], part[4 * c + 1] + mu, part[4 * c + 2], part[4 * c + 3] + both]
        kicked = [w2[4 * c], w2[4 * c + 1] + dt2 * mu, w2[4 * c + 2], w2[4 * c + 3] + dt2 * both]
        f2[2 * c] = forces[1]
        f2[2 * c + 1] = forces[3]
        totals = gathered(totals, products(forces, LATE) + products(kicked, LATE))
    sums[...] = early[...] + lanes_of(totals, N_EARLY)


def form(coefficients, basis):
    total = None
    for (i, j), term in coefficients.items():
        for b in basis[i] + basis[j]:
            term = term * b
        if i != j:
            term = 2.0 * term
        total = term if total is None else total + term
    return jnp.maximum(total, 0.0)


def ratio(kicked, force):
    return jnp.sqrt(kicked / (force + 1e-06))


def last_kernel(dts, marks, parts, u, v, p, g, part, f2, pos, vel):
    rows = pos.shape[1]
    sums = jnp.sum(parts[...], axis=0)
    lanes = [sums[:, i : i + 1] for i in range(N_EARLY + N_LATE)]

    def take(pairs, at):
        return {pair: lanes[at + i] for i, pair in enumerate(pairs)}

    dt0, dt1, dt2 = dts[0], dts[1], dts[2]
    kappa = 1.0 - gamma()
    c0 = ratio(lanes[1], lanes[0])
    mu = kappa * dt0 + gamma() * c0
    one = ((), (mu,))
    c1 = ratio(form(take(all_pairs(2), 5), one), form(take(all_pairs(2), 2), one))
    two = ((), (mu,), (c1,), (mu, c1))
    force_sq = take(EARLY, 8) | take(LATE, N_EARLY)
    kicked_sq = take(EARLY, 8 + len(EARLY)) | take(LATE, N_EARLY + len(LATE))
    c2 = ratio(form(kicked_sq, two), form(force_sq, two))
    rho, k1, g1 = weights_of(marks)[0]
    alpha = factors(marks[1], factors(marks[0], jnp.float32(0.1))[0])[0]
    _, k2, g2 = factors(marks[2], alpha)
    for c in range(2):
        f0, h = p[rows * c : rows * c + rows], p[rows * (2 + c) : rows * (2 + c) + rows]
        speed = rho * (kappa * v[c, :rows] + mu * f0)
        field = u[c, :rows] + dt0 * speed
        force = f0 + (dt0 * kappa) * h + (mu * dt0) * g[rows * c : rows * c + rows]
        speed = k1 * (speed + dt1 * force) + (g1 * c1) * force
        field = field + dt1 * speed
        force = part[4 * c] + mu * f2[2 * c] + c1 * (part[4 * c + 2] + mu * f2[2 * c + 1])
        speed = k2 * (speed + dt2 * force) + (g2 * c2) * force
        pos[c] = field + dt2 * speed
        vel[c] = speed


def call(kernel, out_shape, specs, *args, **more):
    return pl.pallas_call(
        kernel,
        out_shape=out_shape,
        in_specs=specs,
        out_specs=jax.tree.map(lambda _: VMEM, out_shape),
        compiler_params=pltpu.CompilerParams(vmem_limit_bytes=40 * 2**20),
        **more,
    )(*args)


def f32(*shape):
    return jax.ShapeDtypeStruct(shape, jnp.float32)


def local(positions, velocity, flow_down, flow_up, flow_mask, resets, dt_index):
    nstrips, nz, nx = lax.axis_size("strip"), lax.axis_size("z"), lax.axis_size("x")
    section, strip = lax.axis_index(GZ), lax.axis_index("strip")
    _, comps, rows, cols = positions.shape
    core = f32(comps, rows, cols)
    marks = (resets[:, 0] == 1).astype(jnp.float32)
    tile = jnp.broadcast_to(jnp.pad(marks, (0, 5))[:, None], (8, cols))
    start = call(
        start_kernel,
        f32(4 * rows + 8, cols),
        [ANY] * 3,
        positions.reshape(-1, cols), velocity.reshape(-1, cols), tile,
        scratch_shapes=[pltpu.SemaphoreType.DMA((3,))],
    )
    even, odd = swap(start, GZ, nz * nx)
    marks = jnp.concatenate([marks] + [x[4 * rows : 4 * rows + 3, 0] for x in (even, odd)])
    dts = 0.1 * jnp.power(jnp.float32(1.25), dt_index.astype(jnp.float32))
    ids = jnp.reshape(strip, (1,))
    is_odd = section % 2 == 1
    valid = jnp.stack([section > 0, section < nz * nx - 1]).astype(jnp.int32)
    masks = (flow_mask[:, 0] * valid[:, None, None]).astype(jnp.float32)
    masks = jnp.where(is_odd, masks, masks[::-1])
    flow_even = jnp.where(is_odd, flow_down[0], flow_up[0])
    flow_odd = jnp.where(is_odd, flow_up[0], flow_down[0])
    own = start[: 4 * rows].reshape(2, comps, rows, cols)
    fields = [own[0], own[1], flow_even, flow_odd, masks]
    size = -(-2 * sum(DEEP) // 8) * 8
    rims = call(
        rims_kernel,
        (f32(size, cols), f32(size, cols)),
        [SMEM] + [VMEM] * 7,
        ids, *fields, even, odd,
    )
    first, second = swap(tuple(rims), "strip", nstrips)
    below = jnp.where(strip % 2 == 1, second, first)
    above = jnp.where(strip % 2 == 1, first, second)
    for x in (even, odd):
        fields += list(x[: 4 * rows].reshape(2, comps, rows, cols))
    wide, at = [], 0
    for f, d in zip(fields, DEEP):
        lower = below[at : at + 2 * d].reshape(2, d, cols)
        upper = above[at : at + 2 * d].reshape(2, d, cols)
        at += 2 * d
        gap = jnp.zeros((2, 8 - 2 * d, cols), jnp.float32)
        wide.append(jnp.concatenate([f, lower, gap, upper], axis=1))
    u, v, fe, fo, mk, ue, ve, uo, vo = wide

    p, ptails = call(
        lambda *refs: first_kernel(nstrips, *refs),
        (f32(4 * rows + 8, cols), f32(32, cols)),
        [SMEM] * 2 + [VMEM] * 9,
        ids, marks, u, ue, uo, v, ve, vo, fe, fo, mk,
    )
    pe, po = swap(p, GZ, nz * nx)
    g, gtails = call(
        lambda *refs: second_kernel(nstrips, *refs),
        (f32(2 * rows + 8, cols), f32(16, cols)),
        [SMEM] * 2 + [VMEM] * 7,
        ids, marks, p, ptails, pe, po, fe, fo, mk,
    )
    ge, go = swap(g, GZ, nz * nx)
    part, w2, early = call(
        lambda *refs: third_kernel(nstrips, *refs),
        (f32(4 * comps, rows, cols), f32(4 * comps, rows, cols), f32(1, 128)),
        [SMEM] * 3 + [VMEM] * 12,
        ids, dts, marks, v, ve, vo, p, ptails, pe, po, g, gtails, fe, fo, mk,
        cost_estimate=pl.CostEstimate(flops=6_000_000, bytes_accessed=4_000_000, transcendentals=0),
    )
    f2, sums = call(
        lambda *refs: fourth_kernel(nstrips, *refs),
        (f32(2 * comps, rows, cols), f32(1, 128)),
        [SMEM] * 3 + [VMEM] * 8,
        ids, dts, marks, part, w2, early, ge, go, fe, fo, mk,
    )
    near = nx * nstrips
    sums = lax.all_to_all(jnp.broadcast_to(sums, (near, 1, 128)), ("x", "strip"), 0, 0)
    sums = jnp.sum(sums, axis=0)
    sums = lax.all_to_all(jnp.broadcast_to(sums, (nz, 1, 128)), "z", 0, 0)
    pos, vel = call(
        last_kernel,
        (core, core),
        [SMEM] * 2 + [VMEM] * 7,
        dts, marks, sums, u, v, p, g, part, f2,
    )
    return pos[None], vel[None]


def solution(mesh):
    sections, strips = mesh.devices.shape
    split = mesh.devices.reshape(sections // X_CHIPS, X_CHIPS, strips)
    field = P(GZ, None, "strip", None)
    placed = (field, field, field, field, P(None, GZ, "strip", None), P(None, GZ), P())
    return jax.shard_map(
        local,
        mesh=Mesh(split, ("z", "x", "strip")),
        in_specs=placed,
        out_specs=(field, field),
        check_vma=False,
    )
```

```python
import jax
import jax.numpy as jnp
from jax import lax
from jax.experimental import pallas as pl
from jax.experimental.pallas import tpu as pltpu
from jax.sharding import Mesh, PartitionSpec as P

GZ = ("z", "x")
X_CHIPS = 4
DEEP = (3, 2, 2, 2, 2, 3, 2, 3, 2)
VMEM = pl.BlockSpec(memory_space=pltpu.VMEM)
SMEM = pl.BlockSpec(memory_space=pltpu.SMEM)
ANY = pl.BlockSpec(memory_space=pl.ANY)


def swap(value, axes, size):
    first = [(i, i ^ 1) for i in range(size)]
    second = [(i, ((i - 1) ^ 1) + 1) for i in range(1, size - 1)]
    values = value if isinstance(value, tuple) else (value, value)
    return lax.ppermute(values[0], axes, first), lax.ppermute(values[1], axes, second)


class Stencil:
    def __init__(self, strip, nstrips, flow_even, flow_odd, mask_even, mask_odd):
        rows, cols = mask_even.shape
        own = rows - 8
        ring = lax.broadcasted_iota(jnp.int32, (rows, 1), 0)
        row = strip * own + jnp.where(ring < own + 4, ring, ring - rows)
        last = nstrips * own - 1
        self.north = jnp.where((row > 0) & (row <= last), 1.0, 0.0).astype(jnp.float32)
        self.south = jnp.where((row >= 0) & (row < last), 1.0, 0.0).astype(jnp.float32)
        col = lax.broadcasted_iota(jnp.int32, (1, cols), 1)
        self.west = jnp.where(col > 0, 1.0, 0.0).astype(jnp.float32)
        self.east = jnp.where(col < cols - 1, 1.0, 0.0).astype(jnp.float32)
        self.flow_even = flow_even
        self.flow_odd = flow_odd
        self.mask_even = mask_even
        self.mask_odd = mask_odd
        degree = (self.north + self.south) + (self.west + self.east)
        self.pull = degree + (mask_even + mask_odd)
        self.rows, self.cols = rows, cols

    def below(self, value):
        return pltpu.roll(value, self.rows - 1, 0)

    def above(self, value):
        return pltpu.roll(value, 1, 0)

    def right(self, value):
        return pltpu.roll(value, self.cols - 1, 1) * self.east

    def left(self, value):
        return pltpu.roll(value, 1, 1) * self.west

    def sample(self, value, flow):
        step = self.right(value) - value
        here = value + flow[1] * step
        lower = self.below(value) + flow[1] * self.below(step)
        return here + flow[0] * (lower - here)

    def inner(self, own):
        total = self.north * self.above(own) + self.south * self.below(own)
        return total + (self.left(own) + self.right(own)) - self.pull * own

    def even(self, value):
        return self.mask_even * self.sample(value, self.flow_even)

    def odd(self, value):
        return self.mask_odd * self.sample(value, self.flow_odd)

    def __call__(self, own, even, odd):
        return self.inner(own) + (self.even(even) + self.odd(odd))

    def bias(self, comp):
        return self.mask_even * self.flow_even[comp] + self.mask_odd * self.flow_odd[comp]


U, V, FE, FO, MK, UE, VE, UO, VO = range(9)


def ring(core, tails, field, c):
    at = 8 * (2 * field + c)
    return jnp.concatenate([core, tails[at : at + 8]], axis=0)


def part(packet, rows, at):
    return packet[rows * at : rows * at + rows]


def stencil_of(ids, nstrips, fe, fo, mk, tails):
    fields = [[ring(x[c], tails, i, c) for c in range(2)] for x, i in ((fe, FE), (fo, FO), (mk, MK))]
    return Stencil(ids[0], nstrips, *fields[:2], *fields[2])


def factors(reset, alpha):
    alpha = jnp.where(reset > 0.5, jnp.float32(0.1), 0.99 * alpha)
    keep = jnp.where(reset > 0.5, jnp.float32(0.0), jnp.float32(1.0))
    return alpha, (1.0 - alpha) * keep, alpha * keep


def gamma():
    return 0.99 * jnp.float32(0.1)


def weights_of(marks):
    weights = []
    for side in range(3):
        alpha = factors(marks[3 * side], jnp.float32(0.1))[0]
        rho = jnp.where(marks[3 * side] > 0.5, jnp.float32(0.0), jnp.float32(1.0))
        weights.append((rho, *factors(marks[3 * side + 1], alpha)[1:]))
    return weights


def start_kernel(rs, pos, vel, out, sems):
    rows = pos.shape[0]
    copies = [
        pltpu.make_async_copy(src, out.at[pl.ds(at, rows)], sems.at[i])
        for i, (src, at) in enumerate(((pos, 0), (vel, rows)))
    ]
    for copy in copies:
        copy.start()
    for i in range(8):
        mark = jnp.where(rs[i] == 1, jnp.float32(1.0), jnp.float32(0.0)) if i < 3 else 0.0
        out[2 * rows + i : 2 * rows + i + 1] = jnp.full((1, out.shape[1]), mark, jnp.float32)
    for copy in copies:
        copy.wait()


def rims_kernel(ids, start, fe, fo, mk, even, odd, first, second):
    rows = fe.shape[1]
    comps = [(start, rows * at) for at in range(4)]
    comps += [(x.at[c], 0) for x in (fe, fo, mk) for c in range(2)]
    comps += [(x, rows * at) for x in (even, odd) for at in range(4)]

    def fill(upper, lower):
        at = 0
        for i, (src, base) in enumerate(comps):
            deep = DEEP[i // 2]
            upper[at : at + deep] = src[base : base + deep]
            lower[at : at + deep] = src[base + rows - deep : base + rows]
            at += deep
        for out in (upper, lower):
            out[at:] = jnp.zeros((out.shape[0] - at, out.shape[1]), jnp.float32)

    @pl.when(ids[0] % 2 == 1)
    def _():
        fill(first, second)

    @pl.when(ids[0] % 2 == 0)
    def _():
        fill(second, first)


def first_kernel(nstrips, ids, start, even, odd, fe, fo, mk, first, second, packet, ftails, tails):
    tails[...] = jnp.zeros(tails.shape, jnp.float32)

    def fill(below, above):
        at = 0
        for i in range(2 * len(DEEP)):
            deep = DEEP[i // 2]
            tails[8 * i : 8 * i + deep] = below[at : at + deep]
            tails[8 * i + 8 - deep : 8 * i + 8] = above[at : at + deep]
            at += deep

    @pl.when(ids[0] % 2 == 1)
    def _():
        fill(second, first)

    @pl.when(ids[0] % 2 == 0)
    def _():
        fill(first, second)

    op = stencil_of(ids, nstrips, fe, fo, mk, tails)
    rows = fe.shape[1]
    end = 2 * rows
    packet[end:] = jnp.zeros((8, packet.shape[1]), jnp.float32)
    for c in range(2):
        us = [ring(part(x, rows, c), tails, i, c) for x, i in ((start, U), (even, UE), (odd, UO))]
        f0 = op(*us) + op.bias(c)
        packet[rows * c : rows * c + rows] = f0[:rows]
        ftails[8 * c : 8 * c + 8] = f0[rows:]
        packet[end + 3 * c : end + 3 * c + 2] = f0[rows : rows + 2]
        last = end + (7, 2)[c]
        packet[last : last + 1] = f0[rows + 7 :]


def velocities(start, even, odd, tails, rows, c):
    return [ring(part(x, rows, 2 + c), tails, i, c) for x, i in ((start, V), (even, VE), (odd, VO))]


def beside_kernel(nstrips, ids, marks, start, even, odd, f, ftails, fe, fo, mk, tails, packet, htails, inner):
    op = stencil_of(ids, nstrips, fe, fo, mk, tails)
    rows = fe.shape[1]
    rhos = [w[0] for w in weights_of(marks)]
    packet[2 * rows :] = jnp.zeros((8, packet.shape[1]), jnp.float32)
    for c in range(2):
        h = op(*[rho * x for rho, x in zip(rhos, velocities(start, even, odd, tails, rows, c))])
        packet[rows * c : rows * c + rows] = h[:rows]
        packet[2 * rows + c : 2 * rows + c + 1] = h[rows : rows + 1]
        htails[8 * c : 8 * c + 8] = h[rows:]
        inner[c] = op.inner(rhos[0] * own_ring(f, ftails, rows, c))


def own_ring(packet, tails, rows, c):
    return ring(part(packet, rows, c), tails, 0, c)


def side_ring(packet, rows, c, step):
    tail = packet[2 * rows :]
    tail = pltpu.roll(tail, 8 - step * c, 0) if c else tail
    return jnp.concatenate([part(packet, rows, c), tail], axis=0)


def second_kernel(nstrips, ids, marks, inner, pe, po, fe, fo, mk, tails, packet, gtails):
    op = stencil_of(ids, nstrips, fe, fo, mk, tails)
    rows = mk.shape[1]
    _, rho_even, rho_odd = [w[0] for w in weights_of(marks)]
    packet[2 * rows :] = jnp.zeros((8, packet.shape[1]), jnp.float32)
    for c in range(2):
        even, odd = side_ring(pe, rows, c, 3), side_ring(po, rows, c, 3)
        g = inner[c] + (rho_even * op.even(even) + rho_odd * op.odd(odd))
        packet[rows * c : rows * c + rows] = g[:rows]
        packet[2 * rows + c : 2 * rows + c + 1] = g[rows : rows + 1]
        gtails[8 * c : 8 * c + 8] = g[rows:]


def products(fields, pairs):
    return [fields[i] * fields[j] for i, j in pairs]


def all_pairs(size):
    return [(i, j) for i in range(size) for j in range(i, size)]


EARLY = [(0, 0), (0, 2), (2, 2)]
LATE = [pair for pair in all_pairs(4) if pair not in EARLY]
N_EARLY = 2 + 3 + 3 + 2 * len(EARLY)
N_LATE = 2 * len(LATE)


def tile_sum(value):
    rows = value.shape[0]
    tall = value[0:8]
    for r in range(8, rows, 8):
        tall = tall + value[r : r + 8]
    total = tall[:, 0:128]
    for col in range(128, value.shape[1], 128):
        total = total + tall[:, col : col + 128]
    return total


def lanes_of(totals, at):
    lane = lax.broadcasted_iota(jnp.int32, (1, 128), 1)
    row = jnp.zeros((1, 128), jnp.float32)
    for i, total in enumerate(totals):
        whole = jnp.sum(jnp.sum(total, axis=0, keepdims=True), axis=1, keepdims=True)
        row = jnp.where(lane == at + i, whole, row)
    return row


def gathered(totals, terms):
    parts = [tile_sum(term) for term in terms]
    return parts if totals is None else [x + y for x, y in zip(totals, parts)]


def third_kernel(nstrips, ids, dts, marks, start, even, odd, f, ftails, pe, po, h, htails, he, ho, g, gtails, fe, fo, mk, tails, f2, w2, sums):
    op = stencil_of(ids, nstrips, fe, fo, mk, tails)
    rows = mk.shape[1]
    dt0, dt1, dt2 = dts[0], dts[1], dts[2]
    kappa = 1.0 - gamma()
    weights = weights_of(marks)
    totals = None
    for c in range(2):
        f0s = [own_ring(f, ftails, rows, c), side_ring(pe, rows, c, 3), side_ring(po, rows, c, 3)]
        hs = [own_ring(h, htails, rows, c), side_ring(he, rows, c, 1), side_ring(ho, rows, c, 1)]
        vs = velocities(start, even, odd, tails, rows, c)
        ts = [x + (dt0 * kappa) * y for x, y in zip(f0s, hs)]
        g0 = dt0 * own_ring(g, gtails, rows, c)
        one = [k1 * ((rho * kappa) * v0 + dt1 * t) for v0, t, (rho, k1, _) in zip(vs, ts, weights)]
        mix = [g1 * t for t, (_, _, g1) in zip(ts, weights)]
        rho, k1, g1 = weights[0]
        mu = k1 * (rho * f0s[0] + dt1 * g0)
        both = g1 * g0
        sides = [(w[1] * w[0]) * x for x, w in zip(f0s[1:], weights[1:])]
        forces = [
            ts[0] + dt1 * op(*one),
            g0 + dt1 * op(mu, *sides),
            dt1 * op(*mix),
            dt1 * op.inner(both),
        ]
        forces = [x[:rows] for x in forces]
        kicked = [x[:rows] + dt2 * y for x, y in zip((one[0], mu, mix[0], both), forces)]
        for i in range(4):
            f2[4 * c + i] = forces[i]
            w2[4 * c + i] = kicked[i]
        f0, v0, t, g0 = f0s[0][:rows], vs[0][:rows], ts[0][:rows], g0[:rows]
        terms = products([f0, v0 + dt0 * f0], [(0, 0), (1, 1)]) + products([t, g0], all_pairs(2))
        terms += products([(rho * kappa) * v0 + dt1 * t, rho * f0 + dt1 * g0], all_pairs(2))
        terms += products(forces, EARLY) + products(kicked, EARLY)
        totals = gathered(totals, terms)
    sums[...] = lanes_of(totals, 0)


def fourth_kernel(nstrips, ids, dts, marks, known, w2, early, ge, go, fe, fo, mk, tails, f2, sums):
    op = stencil_of(ids, nstrips, fe, fo, mk, tails)
    rows = known.shape[1]
    dt0, dt1, dt2 = dts[0], dts[1], dts[2]
    weights = weights_of(marks)
    totals = None
    for c in range(2):
        even = op.even(side_ring(ge, rows, c, 1))[:rows]
        odd = op.odd(side_ring(go, rows, c, 1))[:rows]
        scale = dt1 * dt0
        mu = scale * dt1 * (weights[1][1] * even + weights[2][1] * odd)
        both = scale * (weights[1][2] * even + weights[2][2] * odd)
        forces = [known[4 * c], known[4 * c + 1] + mu, known[4 * c + 2], known[4 * c + 3] + both]
        kicked = [w2[4 * c], w2[4 * c + 1] + dt2 * mu, w2[4 * c + 2], w2[4 * c + 3] + dt2 * both]
        f2[2 * c] = forces[1]
        f2[2 * c + 1] = forces[3]
        totals = gathered(totals, products(forces, LATE) + products(kicked, LATE))
    sums[...] = early[...] + lanes_of(totals, N_EARLY)


def form(coefficients, basis):
    total = None
    for (i, j), term in coefficients.items():
        for b in basis[i] + basis[j]:
            term = term * b
        if i != j:
            term = 2.0 * term
        total = term if total is None else total + term
    return jnp.maximum(total, 0.0)


def ratio(kicked, force):
    return jnp.sqrt(kicked / (force + 1e-06))


def last_kernel(dts, marks, parts, start, f, h, g, known, f2, pos, vel):
    rows = pos.shape[1]
    sums = jnp.sum(parts[...], axis=0)
    lanes = [sums[:, i : i + 1] for i in range(N_EARLY + N_LATE)]

    def take(pairs, at):
        return {pair: lanes[at + i] for i, pair in enumerate(pairs)}

    dt0, dt1, dt2 = dts[0], dts[1], dts[2]
    kappa = 1.0 - gamma()
    c0 = ratio(lanes[1], lanes[0])
    mu = kappa * dt0 + gamma() * c0
    one = ((), (mu,))
    c1 = ratio(form(take(all_pairs(2), 5), one), form(take(all_pairs(2), 2), one))
    two = ((), (mu,), (c1,), (mu, c1))
    force_sq = take(EARLY, 8) | take(LATE, N_EARLY)
    kicked_sq = take(EARLY, 8 + len(EARLY)) | take(LATE, N_EARLY + len(LATE))
    c2 = ratio(form(kicked_sq, two), form(force_sq, two))
    rho, k1, g1 = weights_of(marks)[0]
    alpha = factors(marks[1], factors(marks[0], jnp.float32(0.1))[0])[0]
    _, k2, g2 = factors(marks[2], alpha)
    for c in range(2):
        f0 = part(f, rows, c)
        speed = rho * (kappa * part(start, rows, 2 + c) + mu * f0)
        field = part(start, rows, c) + dt0 * speed
        force = f0 + (dt0 * kappa) * part(h, rows, c) + (mu * dt0) * part(g, rows, c)
        speed = k1 * (speed + dt1 * force) + (g1 * c1) * force
        field = field + dt1 * speed
        force = known[4 * c] + mu * f2[2 * c] + c1 * (known[4 * c + 2] + mu * f2[2 * c + 1])
        speed = k2 * (speed + dt2 * force) + (g2 * c2) * force
        pos[c] = field + dt2 * speed
        vel[c] = speed


def call(kernel, out_shape, specs, *args, room=40 * 2**20, **more):
    return pl.pallas_call(
        kernel,
        out_shape=out_shape,
        in_specs=specs,
        out_specs=jax.tree.map(lambda _: VMEM, out_shape),
        compiler_params=pltpu.CompilerParams(vmem_limit_bytes=room),
        **more,
    )(*args)


def f32(*shape):
    return jax.ShapeDtypeStruct(shape, jnp.float32)


def local(positions, velocity, flow_down, flow_up, flow_mask, resets, dt_index):
    nstrips, nz, nx = lax.axis_size("strip"), lax.axis_size("z"), lax.axis_size("x")
    section, strip = lax.axis_index(GZ), lax.axis_index("strip")
    _, comps, rows, cols = positions.shape
    core = f32(comps, rows, cols)
    marks = (resets[:, 0] == 1).astype(jnp.float32)
    start = call(
        start_kernel,
        f32(4 * rows + 8, cols),
        [SMEM] + [ANY] * 2,
        resets[:, 0], positions.reshape(-1, cols), velocity.reshape(-1, cols),
        room=None,
        scratch_shapes=[pltpu.SemaphoreType.DMA((2,))],
    )
    even, odd = swap(start, GZ, nz * nx)
    marks = jnp.concatenate([marks] + [x[4 * rows : 4 * rows + 3, 0] for x in (even, odd)])
    dts = 0.1 * jnp.power(jnp.float32(1.25), dt_index.astype(jnp.float32))
    ids = jnp.reshape(strip, (1,))
    is_odd = section % 2 == 1
    valid = jnp.stack([section > 0, section < nz * nx - 1]).astype(jnp.int32)
    masks = (flow_mask[:, 0] * valid[:, None, None]).astype(jnp.float32)
    masks = jnp.where(is_odd, masks, masks[::-1])
    flow_even = jnp.where(is_odd, flow_down[0], flow_up[0])
    flow_odd = jnp.where(is_odd, flow_up[0], flow_down[0])
    size = -(-2 * sum(DEEP) // 8) * 8
    rims = call(
        rims_kernel,
        (f32(size, cols), f32(size, cols)),
        [SMEM] + [VMEM] * 6,
        ids, start, flow_even, flow_odd, masks, even, odd,
    )
    first, second = swap(tuple(rims), "strip", nstrips)
    statics = (flow_even, flow_odd, masks)
    side_by_side = pl.CostEstimate(flops=4_000_000, bytes_accessed=3_000_000, transcendentals=0)
    packet = f32(2 * rows + 8, cols)
    ends = (start, even, odd)
    f, ftails, tails = call(
        lambda *refs: first_kernel(nstrips, *refs),
        (packet, f32(16, cols), f32(16 * len(DEEP), cols)),
        [SMEM] + [VMEM] * 8,
        ids, *ends, *statics, first, second,
    )
    pe, po = swap(f, GZ, nz * nx)
    h, htails, inner = call(
        lambda *refs: beside_kernel(nstrips, *refs),
        (packet, f32(16, cols), f32(comps, rows + 8, cols)),
        [SMEM] * 2 + [VMEM] * 9,
        ids, marks, *ends, f, ftails, *statics, tails,
        cost_estimate=side_by_side,
    )
    he, ho = swap(h, GZ, nz * nx)
    g, gtails = call(
        lambda *refs: second_kernel(nstrips, *refs),
        (packet, f32(16, cols)),
        [SMEM] * 2 + [VMEM] * 7,
        ids, marks, inner, pe, po, *statics, tails,
    )
    ge, go = swap(g, GZ, nz * nx)
    known, w2, early = call(
        lambda *refs: third_kernel(nstrips, *refs),
        (f32(4 * comps, rows, cols), f32(4 * comps, rows, cols), f32(1, 128)),
        [SMEM] * 3 + [VMEM] * 17,
        ids, dts, marks, *ends, f, ftails, pe, po, h, htails, he, ho, g, gtails, *statics, tails,
        cost_estimate=side_by_side,
    )
    f2, sums = call(
        lambda *refs: fourth_kernel(nstrips, *refs),
        (f32(2 * comps, rows, cols), f32(1, 128)),
        [SMEM] * 3 + [VMEM] * 9,
        ids, dts, marks, known, w2, early, ge, go, *statics, tails,
    )
    near = nx * nstrips
    sums = lax.all_to_all(jnp.broadcast_to(sums, (near, 1, 128)), ("x", "strip"), 0, 0)
    sums = jnp.sum(sums, axis=0)
    sums = lax.all_to_all(jnp.broadcast_to(sums, (nz, 1, 128)), "z", 0, 0)
    pos, vel = call(
        last_kernel,
        (core, core),
        [SMEM] * 2 + [VMEM] * 7,
        dts, marks, sums, start, f, h, g, known, f2,
    )
    return pos[None], vel[None]


def solution(mesh):
    sections, strips = mesh.devices.shape
    split = mesh.devices.reshape(sections // X_CHIPS, X_CHIPS, strips)
    field = P(GZ, None, "strip", None)
    placed = (field, field, field, field, P(None, GZ, "strip", None), P(None, GZ), P())
    return jax.shard_map(
        local,
        mesh=Mesh(split, ("z", "x", "strip")),
        in_specs=placed,
        out_specs=(field, field),
        check_vma=False,
    )
```

```python
import jax
import jax.numpy as jnp
from jax import lax
from jax.experimental import pallas as pl
from jax.experimental.pallas import tpu as pltpu
from jax.sharding import Mesh, PartitionSpec as P

GZ = ("z", "x")
X_CHIPS = 4
DEEP = (3, 2, 2, 2, 2, 3, 2, 3, 2)
VMEM = pl.BlockSpec(memory_space=pltpu.VMEM)
SMEM = pl.BlockSpec(memory_space=pltpu.SMEM)
ANY = pl.BlockSpec(memory_space=pl.ANY)


def swap(value, axes, size):
    first = [(i, i ^ 1) for i in range(size)]
    second = [(i, ((i - 1) ^ 1) + 1) for i in range(1, size - 1)]
    values = value if isinstance(value, tuple) else (value, value)
    return lax.ppermute(values[0], axes, first), lax.ppermute(values[1], axes, second)


class Stencil:
    def __init__(self, strip, nstrips, flow_even, flow_odd, mask_even, mask_odd):
        rows, cols = mask_even.shape
        own = rows - 8
        ring = lax.broadcasted_iota(jnp.int32, (rows, 1), 0)
        row = strip * own + jnp.where(ring < own + 4, ring, ring - rows)
        last = nstrips * own - 1
        self.north = jnp.where((row > 0) & (row <= last), 1.0, 0.0).astype(jnp.float32)
        self.south = jnp.where((row >= 0) & (row < last), 1.0, 0.0).astype(jnp.float32)
        col = lax.broadcasted_iota(jnp.int32, (1, cols), 1)
        self.west = jnp.where(col > 0, 1.0, 0.0).astype(jnp.float32)
        self.east = jnp.where(col < cols - 1, 1.0, 0.0).astype(jnp.float32)
        self.flow_even = flow_even
        self.flow_odd = flow_odd
        self.mask_even = mask_even
        self.mask_odd = mask_odd
        degree = (self.north + self.south) + (self.west + self.east)
        self.pull = degree + (mask_even + mask_odd)
        self.rows, self.cols = rows, cols

    def below(self, value):
        return pltpu.roll(value, self.rows - 1, 0)

    def above(self, value):
        return pltpu.roll(value, 1, 0)

    def right(self, value):
        return pltpu.roll(value, self.cols - 1, 1) * self.east

    def left(self, value):
        return pltpu.roll(value, 1, 1) * self.west

    def sample(self, value, flow):
        step = self.right(value) - value
        here = value + flow[1] * step
        lower = self.below(value) + flow[1] * self.below(step)
        return here + flow[0] * (lower - here)

    def inner(self, own):
        total = self.north * self.above(own) + self.south * self.below(own)
        return total + (self.left(own) + self.right(own)) - self.pull * own

    def even(self, value):
        return self.mask_even * self.sample(value, self.flow_even)

    def odd(self, value):
        return self.mask_odd * self.sample(value, self.flow_odd)

    def __call__(self, own, even, odd):
        return self.inner(own) + (self.even(even) + self.odd(odd))

    def bias(self, comp):
        return self.mask_even * self.flow_even[comp] + self.mask_odd * self.flow_odd[comp]


U, V, FE, FO, MK, UE, VE, UO, VO = range(9)


def ring(core, tails, field, c):
    at = 8 * (2 * field + c)
    return jnp.concatenate([core, tails[at : at + 8]], axis=0)


def part(packet, rows, at):
    return packet[rows * at : rows * at + rows]


def stencil_of(ids, nstrips, fe, fo, mk, tails):
    fields = [[ring(x[c], tails, i, c) for c in range(2)] for x, i in ((fe, FE), (fo, FO), (mk, MK))]
    return Stencil(ids[0], nstrips, *fields[:2], *fields[2])


def factors(reset, alpha):
    alpha = jnp.where(reset > 0.5, jnp.float32(0.1), 0.99 * alpha)
    keep = jnp.where(reset > 0.5, jnp.float32(0.0), jnp.float32(1.0))
    return alpha, (1.0 - alpha) * keep, alpha * keep


def gamma():
    return 0.99 * jnp.float32(0.1)


def weights_of(marks):
    weights = []
    for side in range(3):
        alpha = factors(marks[3 * side], jnp.float32(0.1))[0]
        rho = jnp.where(marks[3 * side] > 0.5, jnp.float32(0.0), jnp.float32(1.0))
        weights.append((rho, *factors(marks[3 * side + 1], alpha)[1:]))
    return weights


def start_kernel(resets, pos, vel, out, rs, sems):
    rows = pos.shape[0]
    moves = ((resets, rs), (pos, out.at[pl.ds(0, rows)]), (vel, out.at[pl.ds(rows, rows)]))
    copies = [pltpu.make_async_copy(src, dst, sems.at[i]) for i, (src, dst) in enumerate(moves)]
    for copy in copies:
        copy.start()
    out[2 * rows :] = jnp.zeros((8, out.shape[1]), jnp.float32)
    copies[0].wait()
    for i in range(3):
        mark = jnp.where(rs[i] == 1, jnp.float32(1.0), jnp.float32(0.0))
        out[2 * rows + i : 2 * rows + i + 1] = jnp.full((1, out.shape[1]), mark, jnp.float32)
    for copy in copies[1:]:
        copy.wait()


def rims_kernel(ids, start, fe, fo, mk, even, odd, first, second):
    rows = fe.shape[1]
    comps = [(start, rows * at) for at in range(4)]
    comps += [(x.at[c], 0) for x in (fe, fo, mk) for c in range(2)]
    comps += [(x, rows * at) for x in (even, odd) for at in range(4)]

    def fill(upper, lower):
        at = 0
        for i, (src, base) in enumerate(comps):
            deep = DEEP[i // 2]
            upper[at : at + deep] = src[base : base + deep]
            lower[at : at + deep] = src[base + rows - deep : base + rows]
            at += deep
        for out in (upper, lower):
            out[at:] = jnp.zeros((out.shape[0] - at, out.shape[1]), jnp.float32)

    @pl.when(ids[0] % 2 == 1)
    def _():
        fill(first, second)

    @pl.when(ids[0] % 2 == 0)
    def _():
        fill(second, first)


def first_kernel(nstrips, ids, start, even, odd, fe, fo, mk, second, first, packet, ftails, tails):
    tails[...] = jnp.zeros(tails.shape, jnp.float32)

    def fill(below, above):
        at = 0
        for i in range(2 * len(DEEP)):
            deep = DEEP[i // 2]
            tails[8 * i : 8 * i + deep] = below[at : at + deep]
            tails[8 * i + 8 - deep : 8 * i + 8] = above[at : at + deep]
            at += deep

    @pl.when(ids[0] % 2 == 1)
    def _():
        fill(second, first)

    @pl.when(ids[0] % 2 == 0)
    def _():
        fill(first, second)

    op = stencil_of(ids, nstrips, fe, fo, mk, tails)
    rows = fe.shape[1]
    end = 2 * rows
    packet[end:] = jnp.zeros((8, packet.shape[1]), jnp.float32)
    for c in range(2):
        us = [ring(part(x, rows, c), tails, i, c) for x, i in ((start, U), (even, UE), (odd, UO))]
        f0 = op(*us) + op.bias(c)
        packet[rows * c : rows * c + rows] = f0[:rows]
        ftails[8 * c : 8 * c + 8] = f0[rows:]
        packet[end + 3 * c : end + 3 * c + 2] = f0[rows : rows + 2]
        last = end + (7, 2)[c]
        packet[last : last + 1] = f0[rows + 7 :]


def velocities(start, even, odd, tails, rows, c):
    return [ring(part(x, rows, 2 + c), tails, i, c) for x, i in ((start, V), (even, VE), (odd, VO))]


def beside_kernel(nstrips, ids, marks, start, even, odd, f, ftails, fe, fo, mk, tails, packet, htails, inner):
    op = stencil_of(ids, nstrips, fe, fo, mk, tails)
    rows = fe.shape[1]
    rhos = [w[0] for w in weights_of(marks)]
    packet[2 * rows :] = jnp.zeros((8, packet.shape[1]), jnp.float32)
    for c in range(2):
        h = op(*[rho * x for rho, x in zip(rhos, velocities(start, even, odd, tails, rows, c))])
        packet[rows * c : rows * c + rows] = h[:rows]
        packet[2 * rows + c : 2 * rows + c + 1] = h[rows : rows + 1]
        htails[8 * c : 8 * c + 8] = h[rows:]
        inner[c] = op.inner(rhos[0] * own_ring(f, ftails, rows, c))


def own_ring(packet, tails, rows, c):
    return ring(part(packet, rows, c), tails, 0, c)


def side_ring(packet, rows, c, step):
    tail = packet[2 * rows :]
    tail = pltpu.roll(tail, 8 - step * c, 0) if c else tail
    return jnp.concatenate([part(packet, rows, c), tail], axis=0)


def second_kernel(nstrips, ids, marks, inner, pe, po, fe, fo, mk, tails, packet, gtails):
    op = stencil_of(ids, nstrips, fe, fo, mk, tails)
    rows = mk.shape[1]
    _, rho_even, rho_odd = [w[0] for w in weights_of(marks)]
    packet[2 * rows :] = jnp.zeros((8, packet.shape[1]), jnp.float32)
    for c in range(2):
        even, odd = side_ring(pe, rows, c, 3), side_ring(po, rows, c, 3)
        g = inner[c] + (rho_even * op.even(even) + rho_odd * op.odd(odd))
        packet[rows * c : rows * c + rows] = g[:rows]
        packet[2 * rows + c : 2 * rows + c + 1] = g[rows : rows + 1]
        gtails[8 * c : 8 * c + 8] = g[rows:]


def products(fields, pairs):
    return [fields[i] * fields[j] for i, j in pairs]


def all_pairs(size):
    return [(i, j) for i in range(size) for j in range(i, size)]


EARLY = [(0, 0), (0, 2), (2, 2)]
LATE = [pair for pair in all_pairs(4) if pair not in EARLY]
N_EARLY = 2 + 3 + 3 + 2 * len(EARLY)
N_LATE = 2 * len(LATE)


def tile_sum(value):
    rows = value.shape[0]
    tall = value[0:8]
    for r in range(8, rows, 8):
        tall = tall + value[r : r + 8]
    total = tall[:, 0:128]
    for col in range(128, value.shape[1], 128):
        total = total + tall[:, col : col + 128]
    return total


def lanes_of(totals, at):
    lane = lax.broadcasted_iota(jnp.int32, (1, 128), 1)
    row = jnp.zeros((1, 128), jnp.float32)
    for i, total in enumerate(totals):
        whole = jnp.sum(jnp.sum(total, axis=0, keepdims=True), axis=1, keepdims=True)
        row = jnp.where(lane == at + i, whole, row)
    return row


def gathered(totals, terms):
    parts = [tile_sum(term) for term in terms]
    return parts if totals is None else [x + y for x, y in zip(totals, parts)]


def third_kernel(nstrips, ids, dts, marks, start, even, odd, f, ftails, pe, po, h, htails, he, ho, g, gtails, fe, fo, mk, tails, f2, w2, sums):
    op = stencil_of(ids, nstrips, fe, fo, mk, tails)
    rows = mk.shape[1]
    dt0, dt1, dt2 = dts[0], dts[1], dts[2]
    kappa = 1.0 - gamma()
    weights = weights_of(marks)
    totals = None
    for c in range(2):
        f0s = [own_ring(f, ftails, rows, c), side_ring(pe, rows, c, 3), side_ring(po, rows, c, 3)]
        hs = [own_ring(h, htails, rows, c), side_ring(he, rows, c, 1), side_ring(ho, rows, c, 1)]
        vs = velocities(start, even, odd, tails, rows, c)
        ts = [x + (dt0 * kappa) * y for x, y in zip(f0s, hs)]
        g0 = dt0 * own_ring(g, gtails, rows, c)
        one = [k1 * ((rho * kappa) * v0 + dt1 * t) for v0, t, (rho, k1, _) in zip(vs, ts, weights)]
        mix = [g1 * t for t, (_, _, g1) in zip(ts, weights)]
        rho, k1, g1 = weights[0]
        mu = k1 * (rho * f0s[0] + dt1 * g0)
        both = g1 * g0
        sides = [(w[1] * w[0]) * x for x, w in zip(f0s[1:], weights[1:])]
        forces = [
            ts[0] + dt1 * op(*one),
            g0 + dt1 * op(mu, *sides),
            dt1 * op(*mix),
            dt1 * op.inner(both),
        ]
        forces = [x[:rows] for x in forces]
        kicked = [x[:rows] + dt2 * y for x, y in zip((one[0], mu, mix[0], both), forces)]
        for i in range(4):
            f2[4 * c + i] = forces[i]
            w2[4 * c + i] = kicked[i]
        f0, v0, t, g0 = f0s[0][:rows], vs[0][:rows], ts[0][:rows], g0[:rows]
        terms = products([f0, v0 + dt0 * f0], [(0, 0), (1, 1)]) + products([t, g0], all_pairs(2))
        terms += products([(rho * kappa) * v0 + dt1 * t, rho * f0 + dt1 * g0], all_pairs(2))
        terms += products(forces, EARLY) + products(kicked, EARLY)
        totals = gathered(totals, terms)
    sums[...] = lanes_of(totals, 0)


def fourth_kernel(nstrips, ids, dts, marks, known, w2, early, ge, go, fe, fo, mk, tails, f2, sums):
    op = stencil_of(ids, nstrips, fe, fo, mk, tails)
    rows = known.shape[1]
    dt0, dt1, dt2 = dts[0], dts[1], dts[2]
    weights = weights_of(marks)
    totals = None
    for c in range(2):
        even = op.even(side_ring(ge, rows, c, 1))[:rows]
        odd = op.odd(side_ring(go, rows, c, 1))[:rows]
        scale = dt1 * dt0
        mu = scale * dt1 * (weights[1][1] * even + weights[2][1] * odd)
        both = scale * (weights[1][2] * even + weights[2][2] * odd)
        forces = [known[4 * c], known[4 * c + 1] + mu, known[4 * c + 2], known[4 * c + 3] + both]
        kicked = [w2[4 * c], w2[4 * c + 1] + dt2 * mu, w2[4 * c + 2], w2[4 * c + 3] + dt2 * both]
        f2[2 * c] = forces[1]
        f2[2 * c + 1] = forces[3]
        totals = gathered(totals, products(forces, LATE) + products(kicked, LATE))
    sums[...] = early[...] + lanes_of(totals, N_EARLY)


def form(coefficients, basis):
    total = None
    for (i, j), term in coefficients.items():
        for b in basis[i] + basis[j]:
            term = term * b
        if i != j:
            term = 2.0 * term
        total = term if total is None else total + term
    return jnp.maximum(total, 0.0)


def ratio(kicked, force):
    return jnp.sqrt(kicked / (force + 1e-06))


def last_kernel(dts, marks, parts, start, f, h, g, known, f2, pos, vel, done, sems):
    rows = pos.shape[1]
    copies = []
    sums = jnp.sum(parts[...], axis=0)
    lanes = [sums[:, i : i + 1] for i in range(N_EARLY + N_LATE)]

    def take(pairs, at):
        return {pair: lanes[at + i] for i, pair in enumerate(pairs)}

    dt0, dt1, dt2 = dts[0], dts[1], dts[2]
    kappa = 1.0 - gamma()
    c0 = ratio(lanes[1], lanes[0])
    mu = kappa * dt0 + gamma() * c0
    one = ((), (mu,))
    c1 = ratio(form(take(all_pairs(2), 5), one), form(take(all_pairs(2), 2), one))
    two = ((), (mu,), (c1,), (mu, c1))
    force_sq = take(EARLY, 8) | take(LATE, N_EARLY)
    kicked_sq = take(EARLY, 8 + len(EARLY)) | take(LATE, N_EARLY + len(LATE))
    c2 = ratio(form(kicked_sq, two), form(force_sq, two))
    rho, k1, g1 = weights_of(marks)[0]
    alpha = factors(marks[1], factors(marks[0], jnp.float32(0.1))[0])[0]
    _, k2, g2 = factors(marks[2], alpha)
    for c in range(2):
        f0 = part(f, rows, c)
        speed = rho * (kappa * part(start, rows, 2 + c) + mu * f0)
        field = part(start, rows, c) + dt0 * speed
        force = f0 + (dt0 * kappa) * part(h, rows, c) + (mu * dt0) * part(g, rows, c)
        speed = k1 * (speed + dt1 * force) + (g1 * c1) * force
        field = field + dt1 * speed
        force = known[4 * c] + mu * f2[2 * c] + c1 * (known[4 * c + 2] + mu * f2[2 * c + 1])
        speed = k2 * (speed + dt2 * force) + (g2 * c2) * force
        done[0, c] = field + dt2 * speed
        done[1, c] = speed
        for i, out in enumerate((pos, vel)):
            copies.append(pltpu.make_async_copy(done.at[i, c], out.at[c], sems.at[i, c]))
            copies[-1].start()
    for copy in copies:
        copy.wait()


def call(kernel, out_shape, specs, *args, room=40 * 2**20, out_specs=None, **more):
    return pl.pallas_call(
        kernel,
        out_shape=out_shape,
        in_specs=specs,
        out_specs=out_specs or jax.tree.map(lambda _: VMEM, out_shape),
        compiler_params=pltpu.CompilerParams(vmem_limit_bytes=room),
        **more,
    )(*args)


def f32(*shape):
    return jax.ShapeDtypeStruct(shape, jnp.float32)


def local(positions, velocity, flow_down, flow_up, flow_mask, resets, dt_index):
    nstrips, nz, nx = lax.axis_size("strip"), lax.axis_size("z"), lax.axis_size("x")
    section, strip = lax.axis_index(GZ), lax.axis_index("strip")
    _, comps, rows, cols = positions.shape
    core = f32(comps, rows, cols)
    marks = (resets[:, 0] == 1).astype(jnp.float32)
    start = call(
        start_kernel,
        f32(4 * rows + 8, cols),
        [ANY] * 3,
        resets[:, 0], positions.reshape(-1, cols), velocity.reshape(-1, cols),
        room=None,
        scratch_shapes=[pltpu.SMEM((3,), jnp.int32), pltpu.SemaphoreType.DMA((3,))],
    )
    even, odd = swap(start, GZ, nz * nx)
    marks = jnp.concatenate([marks] + [x[4 * rows : 4 * rows + 3, 0] for x in (even, odd)])
    dts = 0.1 * jnp.power(jnp.float32(1.25), dt_index.astype(jnp.float32))
    ids = jnp.reshape(strip, (1,))
    is_odd = section % 2 == 1
    valid = jnp.stack([section > 0, section < nz * nx - 1]).astype(jnp.int32)
    masks = (flow_mask[:, 0] * valid[:, None, None]).astype(jnp.float32)
    masks = jnp.where(is_odd, masks, masks[::-1])
    flow_even = jnp.where(is_odd, flow_down[0], flow_up[0])
    flow_odd = jnp.where(is_odd, flow_up[0], flow_down[0])
    size = -(-2 * sum(DEEP) // 8) * 8
    rims = call(
        rims_kernel,
        (f32(size, cols), f32(size, cols)),
        [SMEM] + [VMEM] * 6,
        ids, start, flow_even, flow_odd, masks, even, odd,
    )
    first, second = swap(tuple(rims), "strip", nstrips)
    statics = (flow_even, flow_odd, masks)
    side_by_side = pl.CostEstimate(flops=4_000_000, bytes_accessed=3_000_000, transcendentals=0)
    packet = f32(2 * rows + 8, cols)
    ends = (start, even, odd)
    f, ftails, tails = call(
        lambda *refs: first_kernel(nstrips, *refs),
        (packet, f32(16, cols), f32(16 * len(DEEP), cols)),
        [SMEM] + [VMEM] * 8,
        ids, *ends, *statics, second, first,
    )
    pe, po = swap(f, GZ, nz * nx)
    h, htails, inner = call(
        lambda *refs: beside_kernel(nstrips, *refs),
        (packet, f32(16, cols), f32(comps, rows + 8, cols)),
        [SMEM] * 2 + [VMEM] * 9,
        ids, marks, *ends, f, ftails, *statics, tails,
        cost_estimate=side_by_side,
    )
    he, ho = swap(h, GZ, nz * nx)
    g, gtails = call(
        lambda *refs: second_kernel(nstrips, *refs),
        (packet, f32(16, cols)),
        [SMEM] * 2 + [VMEM] * 7,
        ids, marks, inner, pe, po, *statics, tails,
    )
    ge, go = swap(g, GZ, nz * nx)
    known, w2, early = call(
        lambda *refs: third_kernel(nstrips, *refs),
        (f32(4 * comps, rows, cols), f32(4 * comps, rows, cols), f32(1, 128)),
        [SMEM] * 3 + [VMEM] * 17,
        ids, dts, marks, *ends, f, ftails, pe, po, h, htails, he, ho, g, gtails, *statics, tails,
        cost_estimate=side_by_side,
    )
    f2, sums = call(
        lambda *refs: fourth_kernel(nstrips, *refs),
        (f32(2 * comps, rows, cols), f32(1, 128)),
        [SMEM] * 3 + [VMEM] * 9,
        ids, dts, marks, known, w2, early, ge, go, *statics, tails,
    )
    near = nx * nstrips
    sums = lax.all_to_all(jnp.broadcast_to(sums, (near, 1, 128)), ("x", "strip"), 0, 0)
    sums = jnp.sum(sums, axis=0)
    sums = lax.all_to_all(jnp.broadcast_to(sums, (nz, 1, 128)), "z", 0, 0)
    pos, vel = call(
        last_kernel,
        (core, core),
        [SMEM] * 2 + [VMEM] * 7,
        dts, marks, sums, start, f, h, g, known, f2,
        out_specs=(ANY, ANY),
        scratch_shapes=[pltpu.VMEM((2, comps, rows, cols), jnp.float32), pltpu.SemaphoreType.DMA((2, comps))],
    )
    return pos[None], vel[None]


def solution(mesh):
    sections, strips = mesh.devices.shape
    split = mesh.devices.reshape(sections // X_CHIPS, X_CHIPS, strips)
    field = P(GZ, None, "strip", None)
    placed = (field, field, field, field, P(None, GZ, "strip", None), P(None, GZ), P())
    return jax.shard_map(
        local,
        mesh=Mesh(split, ("z", "x", "strip")),
        in_specs=placed,
        out_specs=(field, field),
        check_vma=False,
    )
```

```python
import jax
import jax.numpy as jnp
from jax import lax
from jax.experimental import pallas as pl
from jax.experimental.pallas import tpu as pltpu
from jax.sharding import Mesh, PartitionSpec as P

GZ = ("z", "x")
X_CHIPS = 4
DEEP = (3, 2, 2, 2, 2, 3, 2, 3, 2)
VMEM = pl.BlockSpec(memory_space=pltpu.VMEM)
SMEM = pl.BlockSpec(memory_space=pltpu.SMEM)
ANY = pl.BlockSpec(memory_space=pl.ANY)


def swap(value, axes, size):
    first = [(i, i ^ 1) for i in range(size)]
    second = [(i, ((i - 1) ^ 1) + 1) for i in range(1, size - 1)]
    values = value if isinstance(value, tuple) else (value, value)
    return lax.ppermute(values[0], axes, first), lax.ppermute(values[1], axes, second)


class Stencil:
    def __init__(self, strip, nstrips, flow_even, flow_odd, mask_even, mask_odd):
        rows, cols = mask_even.shape
        own = rows - 8
        ring = lax.broadcasted_iota(jnp.int32, (rows, 1), 0)
        row = strip * own + jnp.where(ring < own + 4, ring, ring - rows)
        last = nstrips * own - 1
        self.north = jnp.where((row > 0) & (row <= last), 1.0, 0.0).astype(jnp.float32)
        self.south = jnp.where((row >= 0) & (row < last), 1.0, 0.0).astype(jnp.float32)
        col = lax.broadcasted_iota(jnp.int32, (1, cols), 1)
        self.west = jnp.where(col > 0, 1.0, 0.0).astype(jnp.float32)
        self.east = jnp.where(col < cols - 1, 1.0, 0.0).astype(jnp.float32)
        self.flow_even = flow_even
        self.flow_odd = flow_odd
        self.mask_even = mask_even
        self.mask_odd = mask_odd
        degree = (self.north + self.south) + (self.west + self.east)
        self.pull = degree + (mask_even + mask_odd)
        self.rows, self.cols = rows, cols

    def below(self, value):
        return pltpu.roll(value, self.rows - 1, 0)

    def above(self, value):
        return pltpu.roll(value, 1, 0)

    def right(self, value):
        return pltpu.roll(value, self.cols - 1, 1) * self.east

    def left(self, value):
        return pltpu.roll(value, 1, 1) * self.west

    def sample(self, value, flow):
        step = self.right(value) - value
        here = value + flow[1] * step
        lower = self.below(value) + flow[1] * self.below(step)
        return here + flow[0] * (lower - here)

    def inner(self, own):
        total = self.north * self.above(own) + self.south * self.below(own)
        return total + (self.left(own) + self.right(own)) - self.pull * own

    def even(self, value):
        return self.mask_even * self.sample(value, self.flow_even)

    def odd(self, value):
        return self.mask_odd * self.sample(value, self.flow_odd)

    def __call__(self, own, even, odd):
        return self.inner(own) + (self.even(even) + self.odd(odd))

    def bias(self, comp):
        return self.mask_even * self.flow_even[comp] + self.mask_odd * self.flow_odd[comp]


U, V, FE, FO, MK, UE, VE, UO, VO = range(9)


def ring(core, tails, field, c):
    at = 8 * (2 * field + c)
    return jnp.concatenate([core, tails[at : at + 8]], axis=0)


def part(packet, rows, at):
    return packet[rows * at : rows * at + rows]


def stencil_of(ids, nstrips, fe, fo, mk, tails):
    fields = [[ring(x[c], tails, i, c) for c in range(2)] for x, i in ((fe, FE), (fo, FO), (mk, MK))]
    return Stencil(ids[0], nstrips, *fields[:2], *fields[2])


def factors(reset, alpha):
    alpha = jnp.where(reset > 0.5, jnp.float32(0.1), 0.99 * alpha)
    keep = jnp.where(reset > 0.5, jnp.float32(0.0), jnp.float32(1.0))
    return alpha, (1.0 - alpha) * keep, alpha * keep


def gamma():
    return 0.99 * jnp.float32(0.1)


def weights_of(marks):
    weights = []
    for side in range(3):
        alpha = factors(marks[3 * side], jnp.float32(0.1))[0]
        rho = jnp.where(marks[3 * side] > 0.5, jnp.float32(0.0), jnp.float32(1.0))
        weights.append((rho, *factors(marks[3 * side + 1], alpha)[1:]))
    return weights


def start_kernel(resets, pos, vel, out, rs, sems):
    rows = pos.shape[0]
    moves = ((resets, rs), (pos, out.at[pl.ds(0, rows)]), (vel, out.at[pl.ds(rows, rows)]))
    copies = [pltpu.make_async_copy(src, dst, sems.at[i]) for i, (src, dst) in enumerate(moves)]
    for copy in copies:
        copy.start()
    out[2 * rows :] = jnp.zeros((8, out.shape[1]), jnp.float32)
    copies[0].wait()
    for i in range(3):
        mark = jnp.where(rs[i] == 1, jnp.float32(1.0), jnp.float32(0.0))
        out[2 * rows + i : 2 * rows + i + 1] = jnp.full((1, out.shape[1]), mark, jnp.float32)
    for copy in copies[1:]:
        copy.wait()


def rims_kernel(ids, start, fe, fo, mk, even, odd, first, second):
    rows = fe.shape[1]
    comps = [(start, rows * at) for at in range(4)]
    comps += [(x.at[c], 0) for x in (fe, fo, mk) for c in range(2)]
    comps += [(x, rows * at) for x in (even, odd) for at in range(4)]

    def fill(upper, lower):
        at = 0
        for i, (src, base) in enumerate(comps):
            deep = DEEP[i // 2]
            upper[at : at + deep] = src[base : base + deep]
            lower[at : at + deep] = src[base + rows - deep : base + rows]
            at += deep
        for out in (upper, lower):
            out[at:] = jnp.zeros((out.shape[0] - at, out.shape[1]), jnp.float32)

    @pl.when(ids[0] % 2 == 1)
    def _():
        fill(first, second)

    @pl.when(ids[0] % 2 == 0)
    def _():
        fill(second, first)


def first_kernel(nstrips, ids, start, even, odd, fe, fo, mk, second, first, packet, ftails, tails):
    tails[...] = jnp.zeros(tails.shape, jnp.float32)

    def fill(below, above):
        at = 0
        for i in range(2 * len(DEEP)):
            deep = DEEP[i // 2]
            tails[8 * i : 8 * i + deep] = below[at : at + deep]
            tails[8 * i + 8 - deep : 8 * i + 8] = above[at : at + deep]
            at += deep

    @pl.when(ids[0] % 2 == 1)
    def _():
        fill(second, first)

    @pl.when(ids[0] % 2 == 0)
    def _():
        fill(first, second)

    op = stencil_of(ids, nstrips, fe, fo, mk, tails)
    rows = fe.shape[1]
    end = 2 * rows
    packet[end:] = jnp.zeros((8, packet.shape[1]), jnp.float32)
    for c in range(2):
        us = [ring(part(x, rows, c), tails, i, c) for x, i in ((start, U), (even, UE), (odd, UO))]
        f0 = op(*us) + op.bias(c)
        packet[rows * c : rows * c + rows] = f0[:rows]
        ftails[8 * c : 8 * c + 8] = f0[rows:]
        packet[end + 3 * c : end + 3 * c + 2] = f0[rows : rows + 2]
        last = end + (7, 2)[c]
        packet[last : last + 1] = f0[rows + 7 :]


def velocities(start, even, odd, tails, rows, c):
    return [ring(part(x, rows, 2 + c), tails, i, c) for x, i in ((start, V), (even, VE), (odd, VO))]


def beside_kernel(nstrips, ids, marks, start, even, odd, f, ftails, fe, fo, mk, tails, hs, htails, inner):
    op = stencil_of(ids, nstrips, fe, fo, mk, tails)
    rows = fe.shape[1]
    rhos = [w[0] for w in weights_of(marks)]
    for c in range(2):
        h = op(*[rho * x for rho, x in zip(rhos, velocities(start, even, odd, tails, rows, c))])
        hs[rows * c : rows * c + rows] = h[:rows]
        htails[8 * c : 8 * c + 8] = h[rows:]
        inner[c] = op.inner(rhos[0] * own_ring(f, ftails, rows, c))


def own_ring(packet, tails, rows, c):
    return ring(part(packet, rows, c), tails, 0, c)


def side_ring(packet, rows, at, step):
    tail = packet[packet.shape[0] - 8 :]
    tail = pltpu.roll(tail, 8 - step * at, 0) if at else tail
    return jnp.concatenate([part(packet, rows, at), tail], axis=0)


def second_kernel(nstrips, ids, marks, inner, pe, po, h, htails, fe, fo, mk, tails, packet, gtails):
    op = stencil_of(ids, nstrips, fe, fo, mk, tails)
    rows = mk.shape[1]
    _, rho_even, rho_odd = [w[0] for w in weights_of(marks)]
    end = 4 * rows
    packet[end:] = jnp.zeros((8, packet.shape[1]), jnp.float32)
    packet[2 * rows : end] = h[...]
    for c in range(2):
        packet[end + 2 + c : end + 3 + c] = htails[8 * c : 8 * c + 1]
        even, odd = side_ring(pe, rows, c, 3), side_ring(po, rows, c, 3)
        g = inner[c] + (rho_even * op.even(even) + rho_odd * op.odd(odd))
        packet[rows * c : rows * c + rows] = g[:rows]
        packet[end + c : end + c + 1] = g[rows : rows + 1]
        gtails[8 * c : 8 * c + 8] = g[rows:]


def products(fields, pairs):
    return [fields[i] * fields[j] for i, j in pairs]


def all_pairs(size):
    return [(i, j) for i in range(size) for j in range(i, size)]


N_EARLY = 2 + 3 + 3
N_LATE = 2 * len(all_pairs(4))


def tile_sum(value):
    rows = value.shape[0]
    tall = value[0:8]
    for r in range(8, rows, 8):
        tall = tall + value[r : r + 8]
    total = tall[:, 0:128]
    for col in range(128, value.shape[1], 128):
        total = total + tall[:, col : col + 128]
    return total


def lanes_of(totals, at):
    lane = lax.broadcasted_iota(jnp.int32, (1, 128), 1)
    row = jnp.zeros((1, 128), jnp.float32)
    for i, total in enumerate(totals):
        whole = jnp.sum(jnp.sum(total, axis=0, keepdims=True), axis=1, keepdims=True)
        row = jnp.where(lane == at + i, whole, row)
    return row


def gathered(totals, terms):
    parts = [tile_sum(term) for term in terms]
    return parts if totals is None else [x + y for x, y in zip(totals, parts)]


def third_kernel(nstrips, ids, dts, marks, start, even, odd, f, ftails, pe, po, h, htails, g, gtails, fe, fo, mk, tails, f2, w2, sums):
    op = stencil_of(ids, nstrips, fe, fo, mk, tails)
    rows = mk.shape[1]
    dt0, dt1, dt2 = dts[0], dts[1], dts[2]
    kappa = 1.0 - gamma()
    weights = weights_of(marks)
    totals = None
    for c in range(2):
        f0s = [own_ring(f, ftails, rows, c), side_ring(pe, rows, c, 3), side_ring(po, rows, c, 3)]
        vs = velocities(start, even, odd, tails, rows, c)
        ts = [f0s[0] + (dt0 * kappa) * own_ring(h, htails, rows, c), *f0s[1:]]
        g0 = dt0 * own_ring(g, gtails, rows, c)
        one = [k1 * ((rho * kappa) * v0 + dt1 * t) for v0, t, (rho, k1, _) in zip(vs, ts, weights)]
        mix = [g1 * t for t, (_, _, g1) in zip(ts, weights)]
        rho, k1, g1 = weights[0]
        mu = k1 * (rho * f0s[0] + dt1 * g0)
        both = g1 * g0
        sides = [(w[1] * w[0]) * x for x, w in zip(f0s[1:], weights[1:])]
        forces = [
            ts[0] + dt1 * op(*one),
            g0 + dt1 * op(mu, *sides),
            dt1 * op(*mix),
            dt1 * op.inner(both),
        ]
        forces = [x[:rows] for x in forces]
        kicked = [x[:rows] + dt2 * y for x, y in zip((one[0], mu, mix[0], both), forces)]
        for i in range(4):
            f2[4 * c + i] = forces[i]
            w2[4 * c + i] = kicked[i]
        f0, v0, t, g0 = f0s[0][:rows], vs[0][:rows], ts[0][:rows], g0[:rows]
        terms = products([f0, v0 + dt0 * f0], [(0, 0), (1, 1)]) + products([t, g0], all_pairs(2))
        terms += products([(rho * kappa) * v0 + dt1 * t, rho * f0 + dt1 * g0], all_pairs(2))
        totals = gathered(totals, terms)
    sums[...] = lanes_of(totals, 0)


def fourth_kernel(nstrips, ids, dts, marks, known, w2, early, ge, go, fe, fo, mk, tails, f2, sums):
    op = stencil_of(ids, nstrips, fe, fo, mk, tails)
    rows = known.shape[1]
    dt0, dt1, dt2 = dts[0], dts[1], dts[2]
    (_, k_even, g_even), (_, k_odd, g_odd) = weights_of(marks)[1:]
    totals = None
    for c in range(2):
        keeps, mixes = [], []
        for at, scale in ((2 + c, dt1 * dt0 * (1.0 - gamma())), (c, dt1 * dt0)):
            even = op.even(side_ring(ge, rows, at, 1))[:rows]
            odd = op.odd(side_ring(go, rows, at, 1))[:rows]
            keeps.append((scale * dt1) * (k_even * even + k_odd * odd))
            mixes.append(scale * (g_even * even + g_odd * odd))
        more = keeps + mixes
        forces = [known[4 * c + i] + x for i, x in enumerate(more)]
        kicked = [w2[4 * c + i] + dt2 * x for i, x in enumerate(more)]
        for i, force in enumerate(forces):
            f2[4 * c + i] = force
        totals = gathered(totals, products(forces, all_pairs(4)) + products(kicked, all_pairs(4)))
    sums[...] = early[...] + lanes_of(totals, N_EARLY)


def form(coefficients, basis):
    total = None
    for (i, j), term in coefficients.items():
        for b in basis[i] + basis[j]:
            term = term * b
        if i != j:
            term = 2.0 * term
        total = term if total is None else total + term
    return jnp.maximum(total, 0.0)


def ratio(kicked, force):
    return jnp.sqrt(kicked / (force + 1e-06))


def last_kernel(dts, marks, parts, start, f, g, f2, pos, vel, done, sems):
    rows = pos.shape[1]
    copies = []
    sums = jnp.sum(parts[...], axis=0)
    lanes = [sums[:, i : i + 1] for i in range(N_EARLY + N_LATE)]

    def take(pairs, at):
        return {pair: lanes[at + i] for i, pair in enumerate(pairs)}

    dt0, dt1, dt2 = dts[0], dts[1], dts[2]
    kappa = 1.0 - gamma()
    c0 = ratio(lanes[1], lanes[0])
    mu = kappa * dt0 + gamma() * c0
    one = ((), (mu,))
    c1 = ratio(form(take(all_pairs(2), 5), one), form(take(all_pairs(2), 2), one))
    two = ((), (mu,), (c1,), (mu, c1))
    pairs = all_pairs(4)
    c2 = ratio(form(take(pairs, N_EARLY + len(pairs)), two), form(take(pairs, N_EARLY), two))
    rho, k1, g1 = weights_of(marks)[0]
    alpha = factors(marks[1], factors(marks[0], jnp.float32(0.1))[0])[0]
    _, k2, g2 = factors(marks[2], alpha)
    for c in range(2):
        f0 = part(f, rows, c)
        speed = rho * (kappa * part(start, rows, 2 + c) + mu * f0)
        field = part(start, rows, c) + dt0 * speed
        force = f0 + (dt0 * kappa) * part(g, rows, 2 + c) + (mu * dt0) * part(g, rows, c)
        speed = k1 * (speed + dt1 * force) + (g1 * c1) * force
        field = field + dt1 * speed
        force = f2[4 * c] + mu * f2[4 * c + 1] + c1 * (f2[4 * c + 2] + mu * f2[4 * c + 3])
        speed = k2 * (speed + dt2 * force) + (g2 * c2) * force
        done[0, c] = field + dt2 * speed
        done[1, c] = speed
        for i, out in enumerate((pos, vel)):
            copies.append(pltpu.make_async_copy(done.at[i, c], out.at[c], sems.at[i, c]))
            copies[-1].start()
    for copy in copies:
        copy.wait()


def call(kernel, out_shape, specs, *args, room=40 * 2**20, out_specs=None, **more):
    return pl.pallas_call(
        kernel,
        out_shape=out_shape,
        in_specs=specs,
        out_specs=out_specs or jax.tree.map(lambda _: VMEM, out_shape),
        compiler_params=pltpu.CompilerParams(vmem_limit_bytes=room),
        **more,
    )(*args)


def f32(*shape):
    return jax.ShapeDtypeStruct(shape, jnp.float32)


def local(positions, velocity, flow_down, flow_up, flow_mask, resets, dt_index):
    nstrips, nz, nx = lax.axis_size("strip"), lax.axis_size("z"), lax.axis_size("x")
    section, strip = lax.axis_index(GZ), lax.axis_index("strip")
    _, comps, rows, cols = positions.shape
    core = f32(comps, rows, cols)
    marks = (resets[:, 0] == 1).astype(jnp.float32)
    start = call(
        start_kernel,
        f32(4 * rows + 8, cols),
        [ANY] * 3,
        resets[:, 0], positions.reshape(-1, cols), velocity.reshape(-1, cols),
        room=None,
        scratch_shapes=[pltpu.SMEM((3,), jnp.int32), pltpu.SemaphoreType.DMA((3,))],
    )
    even, odd = swap(start, GZ, nz * nx)
    marks = jnp.concatenate([marks] + [x[4 * rows : 4 * rows + 3, 0] for x in (even, odd)])
    dts = 0.1 * jnp.power(jnp.float32(1.25), dt_index.astype(jnp.float32))
    ids = jnp.reshape(strip, (1,))
    is_odd = section % 2 == 1
    valid = jnp.stack([section > 0, section < nz * nx - 1]).astype(jnp.int32)
    masks = (flow_mask[:, 0] * valid[:, None, None]).astype(jnp.float32)
    masks = jnp.where(is_odd, masks, masks[::-1])
    flow_even = jnp.where(is_odd, flow_down[0], flow_up[0])
    flow_odd = jnp.where(is_odd, flow_up[0], flow_down[0])
    size = -(-2 * sum(DEEP) // 8) * 8
    rims = call(
        rims_kernel,
        (f32(size, cols), f32(size, cols)),
        [SMEM] + [VMEM] * 6,
        ids, start, flow_even, flow_odd, masks, even, odd,
    )
    first, second = swap(tuple(rims), "strip", nstrips)
    statics = (flow_even, flow_odd, masks)
    side_by_side = pl.CostEstimate(flops=4_000_000, bytes_accessed=3_000_000, transcendentals=0)
    packet = f32(2 * rows + 8, cols)
    ends = (start, even, odd)
    f, ftails, tails = call(
        lambda *refs: first_kernel(nstrips, *refs),
        (packet, f32(16, cols), f32(16 * len(DEEP), cols)),
        [SMEM] + [VMEM] * 8,
        ids, *ends, *statics, second, first,
    )
    pe, po = swap(f, GZ, nz * nx)
    h, htails, inner = call(
        lambda *refs: beside_kernel(nstrips, *refs),
        (f32(2 * rows, cols), f32(16, cols), f32(comps, rows + 8, cols)),
        [SMEM] * 2 + [VMEM] * 9,
        ids, marks, *ends, f, ftails, *statics, tails,
        cost_estimate=side_by_side,
    )
    g, gtails = call(
        lambda *refs: second_kernel(nstrips, *refs),
        (f32(4 * rows + 8, cols), f32(16, cols)),
        [SMEM] * 2 + [VMEM] * 9,
        ids, marks, inner, pe, po, h, htails, *statics, tails,
    )
    ge, go = swap(g, GZ, nz * nx)
    known, w2, early = call(
        lambda *refs: third_kernel(nstrips, *refs),
        (f32(4 * comps, rows, cols), f32(4 * comps, rows, cols), f32(1, 128)),
        [SMEM] * 3 + [VMEM] * 15,
        ids, dts, marks, *ends, f, ftails, pe, po, h, htails, g, gtails, *statics, tails,
        cost_estimate=side_by_side,
    )
    f2, sums = call(
        lambda *refs: fourth_kernel(nstrips, *refs),
        (f32(4 * comps, rows, cols), f32(1, 128)),
        [SMEM] * 3 + [VMEM] * 9,
        ids, dts, marks, known, w2, early, ge, go, *statics, tails,
    )
    near = nx * nstrips
    sums = lax.all_to_all(jnp.broadcast_to(sums, (near, 1, 128)), ("x", "strip"), 0, 0)
    sums = jnp.sum(sums, axis=0)
    sums = lax.all_to_all(jnp.broadcast_to(sums, (nz, 1, 128)), "z", 0, 0)
    pos, vel = call(
        last_kernel,
        (core, core),
        [SMEM] * 2 + [VMEM] * 5,
        dts, marks, sums, start, f, g, f2,
        out_specs=(ANY, ANY),
        scratch_shapes=[pltpu.VMEM((2, comps, rows, cols), jnp.float32), pltpu.SemaphoreType.DMA((2, comps))],
    )
    return pos[None], vel[None]


def solution(mesh):
    sections, strips = mesh.devices.shape
    split = mesh.devices.reshape(sections // X_CHIPS, X_CHIPS, strips)
    field = P(GZ, None, "strip", None)
    placed = (field, field, field, field, P(None, GZ, "strip", None), P(None, GZ), P())
    return jax.shard_map(
        local,
        mesh=Mesh(split, ("z", "x", "strip")),
        in_specs=placed,
        out_specs=(field, field),
        check_vma=False,
    )
```

```python
import jax
import jax.numpy as jnp
from jax import lax
from jax.experimental import pallas as pl
from jax.experimental.pallas import tpu as pltpu
from jax.sharding import Mesh, PartitionSpec as P

GZ = ("z", "x")
X_CHIPS = 4
DEEP = (3, 2, 2, 2, 2, 3, 2, 3, 2)
VMEM = pl.BlockSpec(memory_space=pltpu.VMEM)
SMEM = pl.BlockSpec(memory_space=pltpu.SMEM)
ANY = pl.BlockSpec(memory_space=pl.ANY)


def swap(value, axes, size):
    first = [(i, i ^ 1) for i in range(size)]
    second = [(i, ((i - 1) ^ 1) + 1) for i in range(1, size - 1)]
    values = value if isinstance(value, tuple) else (value, value)
    return lax.ppermute(values[0], axes, first), lax.ppermute(values[1], axes, second)


class Stencil:
    def __init__(self, strip, nstrips, flow_even, flow_odd, mask_even, mask_odd):
        rows, cols = mask_even.shape
        own = rows - 8
        ring = lax.broadcasted_iota(jnp.int32, (rows, 1), 0)
        row = strip * own + jnp.where(ring < own + 4, ring, ring - rows)
        last = nstrips * own - 1
        self.north = jnp.where((row > 0) & (row <= last), 1.0, 0.0).astype(jnp.float32)
        self.south = jnp.where((row >= 0) & (row < last), 1.0, 0.0).astype(jnp.float32)
        col = lax.broadcasted_iota(jnp.int32, (1, cols), 1)
        self.west = jnp.where(col > 0, 1.0, 0.0).astype(jnp.float32)
        self.east = jnp.where(col < cols - 1, 1.0, 0.0).astype(jnp.float32)
        self.flow_even = flow_even
        self.flow_odd = flow_odd
        self.mask_even = mask_even
        self.mask_odd = mask_odd
        degree = (self.north + self.south) + (self.west + self.east)
        self.pull = degree + (mask_even + mask_odd)
        self.rows, self.cols = rows, cols

    def below(self, value):
        return pltpu.roll(value, self.rows - 1, 0)

    def above(self, value):
        return pltpu.roll(value, 1, 0)

    def right(self, value):
        return pltpu.roll(value, self.cols - 1, 1) * self.east

    def left(self, value):
        return pltpu.roll(value, 1, 1) * self.west

    def sample(self, value, flow):
        step = self.right(value) - value
        here = value + flow[1] * step
        lower = self.below(value) + flow[1] * self.below(step)
        return here + flow[0] * (lower - here)

    def inner(self, own):
        total = self.north * self.above(own) + self.south * self.below(own)
        return total + (self.left(own) + self.right(own)) - self.pull * own

    def even(self, value):
        return self.mask_even * self.sample(value, self.flow_even)

    def odd(self, value):
        return self.mask_odd * self.sample(value, self.flow_odd)

    def __call__(self, own, even, odd):
        return self.inner(own) + (self.even(even) + self.odd(odd))

    def bias(self, comp):
        return self.mask_even * self.flow_even[comp] + self.mask_odd * self.flow_odd[comp]


U, V, FE, FO, MK, UE, VE, UO, VO = range(9)


def ring(core, tails, field, c):
    at = 8 * (2 * field + c)
    return jnp.concatenate([core, tails[at : at + 8]], axis=0)


def part(packet, rows, at):
    return packet[rows * at : rows * at + rows]


def stencil_of(ids, nstrips, fe, fo, mk, tails):
    fields = [[ring(x[c], tails, i, c) for c in range(2)] for x, i in ((fe, FE), (fo, FO), (mk, MK))]
    return Stencil(ids[0], nstrips, *fields[:2], *fields[2])


def factors(reset, alpha):
    alpha = jnp.where(reset > 0.5, jnp.float32(0.1), 0.99 * alpha)
    keep = jnp.where(reset > 0.5, jnp.float32(0.0), jnp.float32(1.0))
    return alpha, (1.0 - alpha) * keep, alpha * keep


def gamma():
    return 0.99 * jnp.float32(0.1)


def weights_of(marks):
    weights = []
    for side in range(3):
        alpha = factors(marks[3 * side], jnp.float32(0.1))[0]
        rho = jnp.where(marks[3 * side] > 0.5, jnp.float32(0.0), jnp.float32(1.0))
        weights.append((rho, *factors(marks[3 * side + 1], alpha)[1:]))
    return weights


def start_kernel(resets, vel, out, rs, sems):
    rows = vel.shape[0]
    moves = ((resets, rs), (vel, out.at[pl.ds(0, rows)]))
    copies = [pltpu.make_async_copy(src, dst, sems.at[i]) for i, (src, dst) in enumerate(moves)]
    for copy in copies:
        copy.start()
    out[rows:] = jnp.zeros((8, out.shape[1]), jnp.float32)
    copies[0].wait()
    for i in range(3):
        mark = jnp.where(rs[i] == 1, jnp.float32(1.0), jnp.float32(0.0))
        out[rows + i : rows + i + 1] = jnp.full((1, out.shape[1]), mark, jnp.float32)
    for copy in copies[1:]:
        copy.wait()


def rims_kernel(ids, u, v, fe, fo, mk, ue, ve, uo, vo, first, second):
    rows = fe.shape[1]
    comps = [(x, rows * c) for x in (u, v) for c in range(2)]
    comps += [(x.at[c], 0) for x in (fe, fo, mk) for c in range(2)]
    comps += [(x, rows * c) for x in (ue, ve, uo, vo) for c in range(2)]

    def fill(upper, lower):
        at = 0
        for i, (src, base) in enumerate(comps):
            deep = DEEP[i // 2]
            upper[at : at + deep] = src[base : base + deep]
            lower[at : at + deep] = src[base + rows - deep : base + rows]
            at += deep
        for out in (upper, lower):
            out[at:] = jnp.zeros((out.shape[0] - at, out.shape[1]), jnp.float32)

    @pl.when(ids[0] % 2 == 1)
    def _():
        fill(first, second)

    @pl.when(ids[0] % 2 == 0)
    def _():
        fill(second, first)


def first_kernel(nstrips, ids, start, even, odd, fe, fo, mk, second, first, packet, ftails, tails):
    tails[...] = jnp.zeros(tails.shape, jnp.float32)

    def fill(below, above):
        at = 0
        for i in range(2 * len(DEEP)):
            deep = DEEP[i // 2]
            tails[8 * i : 8 * i + deep] = below[at : at + deep]
            tails[8 * i + 8 - deep : 8 * i + 8] = above[at : at + deep]
            at += deep

    @pl.when(ids[0] % 2 == 1)
    def _():
        fill(second, first)

    @pl.when(ids[0] % 2 == 0)
    def _():
        fill(first, second)

    op = stencil_of(ids, nstrips, fe, fo, mk, tails)
    rows = fe.shape[1]
    end = 2 * rows
    packet[end:] = jnp.zeros((8, packet.shape[1]), jnp.float32)
    for c in range(2):
        us = [ring(part(x, rows, c), tails, i, c) for x, i in ((start, U), (even, UE), (odd, UO))]
        f0 = op(*us) + op.bias(c)
        packet[rows * c : rows * c + rows] = f0[:rows]
        ftails[8 * c : 8 * c + 8] = f0[rows:]
        packet[end + 3 * c : end + 3 * c + 2] = f0[rows : rows + 2]
        last = end + (7, 2)[c]
        packet[last : last + 1] = f0[rows + 7 :]


def velocities(start, even, odd, tails, rows, c):
    return [ring(part(x, rows, c), tails, i, c) for x, i in ((start, V), (even, VE), (odd, VO))]


def beside_kernel(nstrips, ids, marks, start, even, odd, f, ftails, fe, fo, mk, tails, packet, htails, inner):
    op = stencil_of(ids, nstrips, fe, fo, mk, tails)
    rows = fe.shape[1]
    rhos = [w[0] for w in weights_of(marks)]
    packet[2 * rows :] = jnp.zeros((8, packet.shape[1]), jnp.float32)
    for c in range(2):
        h = op(*[rho * x for rho, x in zip(rhos, velocities(start, even, odd, tails, rows, c))])
        packet[rows * c : rows * c + rows] = h[:rows]
        packet[2 * rows + c : 2 * rows + c + 1] = h[rows : rows + 1]
        htails[8 * c : 8 * c + 8] = h[rows:]
        inner[c] = op.inner(rhos[0] * own_ring(f, ftails, rows, c))


def own_ring(packet, tails, rows, c):
    return ring(part(packet, rows, c), tails, 0, c)


def side_ring(packet, rows, c, step):
    tail = packet[2 * rows :]
    tail = pltpu.roll(tail, 8 - step * c, 0) if c else tail
    return jnp.concatenate([part(packet, rows, c), tail], axis=0)


def second_kernel(nstrips, ids, marks, inner, pe, po, fe, fo, mk, tails, packet, gtails):
    op = stencil_of(ids, nstrips, fe, fo, mk, tails)
    rows = mk.shape[1]
    _, rho_even, rho_odd = [w[0] for w in weights_of(marks)]
    packet[2 * rows :] = jnp.zeros((8, packet.shape[1]), jnp.float32)
    for c in range(2):
        even, odd = side_ring(pe, rows, c, 3), side_ring(po, rows, c, 3)
        g = inner[c] + (rho_even * op.even(even) + rho_odd * op.odd(odd))
        packet[rows * c : rows * c + rows] = g[:rows]
        packet[2 * rows + c : 2 * rows + c + 1] = g[rows : rows + 1]
        gtails[8 * c : 8 * c + 8] = g[rows:]


def products(fields, pairs):
    return [fields[i] * fields[j] for i, j in pairs]


def all_pairs(size):
    return [(i, j) for i in range(size) for j in range(i, size)]


EARLY = [(0, 0), (0, 2), (2, 2)]
LATE = [pair for pair in all_pairs(4) if pair not in EARLY]
N_EARLY = 2 + 3 + 3 + 2 * len(EARLY)
N_LATE = 2 * len(LATE)


def tile_sum(value):
    rows = value.shape[0]
    tall = value[0:8]
    for r in range(8, rows, 8):
        tall = tall + value[r : r + 8]
    total = tall[:, 0:128]
    for col in range(128, value.shape[1], 128):
        total = total + tall[:, col : col + 128]
    return total


def lanes_of(totals, at):
    lane = lax.broadcasted_iota(jnp.int32, (1, 128), 1)
    row = jnp.zeros((1, 128), jnp.float32)
    for i, total in enumerate(totals):
        whole = jnp.sum(jnp.sum(total, axis=0, keepdims=True), axis=1, keepdims=True)
        row = jnp.where(lane == at + i, whole, row)
    return row


def gathered(totals, terms):
    parts = [tile_sum(term) for term in terms]
    return parts if totals is None else [x + y for x, y in zip(totals, parts)]


def third_kernel(nstrips, ids, dts, marks, start, even, odd, f, ftails, pe, po, h, htails, he, ho, g, gtails, fe, fo, mk, tails, f2, w2, sums):
    op = stencil_of(ids, nstrips, fe, fo, mk, tails)
    rows = mk.shape[1]
    dt0, dt1, dt2 = dts[0], dts[1], dts[2]
    kappa = 1.0 - gamma()
    weights = weights_of(marks)
    totals = None
    for c in range(2):
        f0s = [own_ring(f, ftails, rows, c), side_ring(pe, rows, c, 3), side_ring(po, rows, c, 3)]
        hs = [own_ring(h, htails, rows, c), side_ring(he, rows, c, 1), side_ring(ho, rows, c, 1)]
        vs = velocities(start, even, odd, tails, rows, c)
        ts = [x + (dt0 * kappa) * y for x, y in zip(f0s, hs)]
        g0 = dt0 * own_ring(g, gtails, rows, c)
        one = [k1 * ((rho * kappa) * v0 + dt1 * t) for v0, t, (rho, k1, _) in zip(vs, ts, weights)]
        mix = [g1 * t for t, (_, _, g1) in zip(ts, weights)]
        rho, k1, g1 = weights[0]
        mu = k1 * (rho * f0s[0] + dt1 * g0)
        both = g1 * g0
        sides = [(w[1] * w[0]) * x for x, w in zip(f0s[1:], weights[1:])]
        forces = [
            ts[0] + dt1 * op(*one),
            g0 + dt1 * op(mu, *sides),
            dt1 * op(*mix),
            dt1 * op.inner(both),
        ]
        forces = [x[:rows] for x in forces]
        kicked = [x[:rows] + dt2 * y for x, y in zip((one[0], mu, mix[0], both), forces)]
        for i in range(4):
            f2[4 * c + i] = forces[i]
            w2[4 * c + i] = kicked[i]
        f0, v0, t, g0 = f0s[0][:rows], vs[0][:rows], ts[0][:rows], g0[:rows]
        terms = products([f0, v0 + dt0 * f0], [(0, 0), (1, 1)]) + products([t, g0], all_pairs(2))
        terms += products([(rho * kappa) * v0 + dt1 * t, rho * f0 + dt1 * g0], all_pairs(2))
        terms += products(forces, EARLY) + products(kicked, EARLY)
        totals = gathered(totals, terms)
    sums[...] = lanes_of(totals, 0)


def fourth_kernel(nstrips, ids, dts, marks, known, w2, early, ge, go, fe, fo, mk, tails, f2, sums):
    op = stencil_of(ids, nstrips, fe, fo, mk, tails)
    rows = known.shape[1]
    dt0, dt1, dt2 = dts[0], dts[1], dts[2]
    weights = weights_of(marks)
    totals = None
    for c in range(2):
        even = op.even(side_ring(ge, rows, c, 1))[:rows]
        odd = op.odd(side_ring(go, rows, c, 1))[:rows]
        scale = dt1 * dt0
        mu = scale * dt1 * (weights[1][1] * even + weights[2][1] * odd)
        both = scale * (weights[1][2] * even + weights[2][2] * odd)
        forces = [known[4 * c], known[4 * c + 1] + mu, known[4 * c + 2], known[4 * c + 3] + both]
        kicked = [w2[4 * c], w2[4 * c + 1] + dt2 * mu, w2[4 * c + 2], w2[4 * c + 3] + dt2 * both]
        f2[2 * c] = forces[1]
        f2[2 * c + 1] = forces[3]
        totals = gathered(totals, products(forces, LATE) + products(kicked, LATE))
    sums[...] = early[...] + lanes_of(totals, N_EARLY)


def form(coefficients, basis):
    total = None
    for (i, j), term in coefficients.items():
        for b in basis[i] + basis[j]:
            term = term * b
        if i != j:
            term = 2.0 * term
        total = term if total is None else total + term
    return jnp.maximum(total, 0.0)


def ratio(kicked, force):
    return jnp.sqrt(kicked / (force + 1e-06))


def last_kernel(dts, marks, parts, u, v, f, h, g, known, f2, pos, vel, done, sems):
    rows = pos.shape[1]
    copies = []
    sums = jnp.sum(parts[...], axis=0)
    lanes = [sums[:, i : i + 1] for i in range(N_EARLY + N_LATE)]

    def take(pairs, at):
        return {pair: lanes[at + i] for i, pair in enumerate(pairs)}

    dt0, dt1, dt2 = dts[0], dts[1], dts[2]
    kappa = 1.0 - gamma()
    c0 = ratio(lanes[1], lanes[0])
    mu = kappa * dt0 + gamma() * c0
    one = ((), (mu,))
    c1 = ratio(form(take(all_pairs(2), 5), one), form(take(all_pairs(2), 2), one))
    two = ((), (mu,), (c1,), (mu, c1))
    force_sq = take(EARLY, 8) | take(LATE, N_EARLY)
    kicked_sq = take(EARLY, 8 + len(EARLY)) | take(LATE, N_EARLY + len(LATE))
    c2 = ratio(form(kicked_sq, two), form(force_sq, two))
    rho, k1, g1 = weights_of(marks)[0]
    alpha = factors(marks[1], factors(marks[0], jnp.float32(0.1))[0])[0]
    _, k2, g2 = factors(marks[2], alpha)
    for c in range(2):
        f0 = part(f, rows, c)
        speed = rho * (kappa * part(v, rows, c) + mu * f0)
        field = part(u, rows, c) + dt0 * speed
        force = f0 + (dt0 * kappa) * part(h, rows, c) + (mu * dt0) * part(g, rows, c)
        speed = k1 * (speed + dt1 * force) + (g1 * c1) * force
        field = field + dt1 * speed
        force = known[4 * c] + mu * f2[2 * c] + c1 * (known[4 * c + 2] + mu * f2[2 * c + 1])
        speed = k2 * (speed + dt2 * force) + (g2 * c2) * force
        done[0, c] = field + dt2 * speed
        done[1, c] = speed
        for i, out in enumerate((pos, vel)):
            copies.append(pltpu.make_async_copy(done.at[i, c], out.at[c], sems.at[i, c]))
            copies[-1].start()
    for copy in copies:
        copy.wait()


def call(kernel, out_shape, specs, *args, room=40 * 2**20, out_specs=None, **more):
    return pl.pallas_call(
        kernel,
        out_shape=out_shape,
        in_specs=specs,
        out_specs=out_specs or jax.tree.map(lambda _: VMEM, out_shape),
        compiler_params=pltpu.CompilerParams(vmem_limit_bytes=room),
        **more,
    )(*args)


def f32(*shape):
    return jax.ShapeDtypeStruct(shape, jnp.float32)


def local(positions, velocity, flow_down, flow_up, flow_mask, resets, dt_index):
    nstrips, nz, nx = lax.axis_size("strip"), lax.axis_size("z"), lax.axis_size("x")
    section, strip = lax.axis_index(GZ), lax.axis_index("strip")
    _, comps, rows, cols = positions.shape
    core = f32(comps, rows, cols)
    marks = (resets[:, 0] == 1).astype(jnp.float32)
    u = positions.reshape(-1, cols)
    ue, uo = swap(u, GZ, nz * nx)
    v = call(
        start_kernel,
        f32(2 * rows + 8, cols),
        [ANY] * 2,
        resets[:, 0], velocity.reshape(-1, cols),
        room=None,
        scratch_shapes=[pltpu.SMEM((3,), jnp.int32), pltpu.SemaphoreType.DMA((2,))],
    )
    ve, vo = swap(v, GZ, nz * nx)
    marks = jnp.concatenate([marks] + [x[2 * rows : 2 * rows + 3, 0] for x in (ve, vo)])
    dts = 0.1 * jnp.power(jnp.float32(1.25), dt_index.astype(jnp.float32))
    ids = jnp.reshape(strip, (1,))
    is_odd = section % 2 == 1
    valid = jnp.stack([section > 0, section < nz * nx - 1]).astype(jnp.int32)
    masks = (flow_mask[:, 0] * valid[:, None, None]).astype(jnp.float32)
    masks = jnp.where(is_odd, masks, masks[::-1])
    flow_even = jnp.where(is_odd, flow_down[0], flow_up[0])
    flow_odd = jnp.where(is_odd, flow_up[0], flow_down[0])
    size = -(-2 * sum(DEEP) // 8) * 8
    rims = call(
        rims_kernel,
        (f32(size, cols), f32(size, cols)),
        [SMEM] + [VMEM] * 9,
        ids, u, v, flow_even, flow_odd, masks, ue, ve, uo, vo,
    )
    first, second = swap(tuple(rims), "strip", nstrips)
    statics = (flow_even, flow_odd, masks)
    side_by_side = pl.CostEstimate(flops=4_000_000, bytes_accessed=3_000_000, transcendentals=0)
    packet = f32(2 * rows + 8, cols)
    speeds = (v, ve, vo)
    f, ftails, tails = call(
        lambda *refs: first_kernel(nstrips, *refs),
        (packet, f32(16, cols), f32(16 * len(DEEP), cols)),
        [SMEM] + [VMEM] * 8,
        ids, u, ue, uo, *statics, second, first,
    )
    pe, po = swap(f, GZ, nz * nx)
    h, htails, inner = call(
        lambda *refs: beside_kernel(nstrips, *refs),
        (packet, f32(16, cols), f32(comps, rows + 8, cols)),
        [SMEM] * 2 + [VMEM] * 9,
        ids, marks, *speeds, f, ftails, *statics, tails,
        cost_estimate=side_by_side,
    )
    he, ho = swap(h, GZ, nz * nx)
    g, gtails = call(
        lambda *refs: second_kernel(nstrips, *refs),
        (packet, f32(16, cols)),
        [SMEM] * 2 + [VMEM] * 7,
        ids, marks, inner, pe, po, *statics, tails,
    )
    ge, go = swap(g, GZ, nz * nx)
    known, w2, early = call(
        lambda *refs: third_kernel(nstrips, *refs),
        (f32(4 * comps, rows, cols), f32(4 * comps, rows, cols), f32(1, 128)),
        [SMEM] * 3 + [VMEM] * 17,
        ids, dts, marks, *speeds, f, ftails, pe, po, h, htails, he, ho, g, gtails, *statics, tails,
        cost_estimate=side_by_side,
    )
    f2, sums = call(
        lambda *refs: fourth_kernel(nstrips, *refs),
        (f32(2 * comps, rows, cols), f32(1, 128)),
        [SMEM] * 3 + [VMEM] * 9,
        ids, dts, marks, known, w2, early, ge, go, *statics, tails,
    )
    near = nx * nstrips
    sums = lax.all_to_all(jnp.broadcast_to(sums, (near, 1, 128)), ("x", "strip"), 0, 0)
    sums = jnp.sum(sums, axis=0)
    sums = lax.all_to_all(jnp.broadcast_to(sums, (nz, 1, 128)), "z", 0, 0)
    pos, vel = call(
        last_kernel,
        (core, core),
        [SMEM] * 2 + [VMEM] * 8,
        dts, marks, sums, u, v, f, h, g, known, f2,
        out_specs=(ANY, ANY),
        scratch_shapes=[pltpu.VMEM((2, comps, rows, cols), jnp.float32), pltpu.SemaphoreType.DMA((2, comps))],
    )
    return pos[None], vel[None]


def solution(mesh):
    sections, strips = mesh.devices.shape
    split = mesh.devices.reshape(sections // X_CHIPS, X_CHIPS, strips)
    field = P(GZ, None, "strip", None)
    placed = (field, field, field, field, P(None, GZ, "strip", None), P(None, GZ), P())
    return jax.shard_map(
        local,
        mesh=Mesh(split, ("z", "x", "strip")),
        in_specs=placed,
        out_specs=(field, field),
        check_vma=False,
    )
```

```python
import jax
import jax.numpy as jnp
from jax import lax
from jax.experimental import pallas as pl
from jax.experimental.pallas import tpu as pltpu
from jax.sharding import Mesh, PartitionSpec as P

GZ = ("z", "x")
X_CHIPS = 4
DEEP = (3, 2, 2, 2, 2, 3, 2, 3, 2)
VMEM = pl.BlockSpec(memory_space=pltpu.VMEM)
SMEM = pl.BlockSpec(memory_space=pltpu.SMEM)
ANY = pl.BlockSpec(memory_space=pl.ANY)


def swap(value, axes, size):
    first = [(i, i ^ 1) for i in range(size)]
    second = [(i, ((i - 1) ^ 1) + 1) for i in range(1, size - 1)]
    values = value if isinstance(value, tuple) else (value, value)
    return lax.ppermute(values[0], axes, first), lax.ppermute(values[1], axes, second)


class Stencil:
    def __init__(self, strip, nstrips, flow_even, flow_odd, mask_even, mask_odd):
        rows, cols = mask_even.shape
        own = rows - 8
        ring = lax.broadcasted_iota(jnp.int32, (rows, 1), 0)
        row = strip * own + jnp.where(ring < own + 4, ring, ring - rows)
        last = nstrips * own - 1
        self.north = jnp.where((row > 0) & (row <= last), 1.0, 0.0).astype(jnp.float32)
        self.south = jnp.where((row >= 0) & (row < last), 1.0, 0.0).astype(jnp.float32)
        col = lax.broadcasted_iota(jnp.int32, (1, cols), 1)
        self.west = jnp.where(col > 0, 1.0, 0.0).astype(jnp.float32)
        self.east = jnp.where(col < cols - 1, 1.0, 0.0).astype(jnp.float32)
        self.flow_even = flow_even
        self.flow_odd = flow_odd
        self.mask_even = mask_even
        self.mask_odd = mask_odd
        degree = (self.north + self.south) + (self.west + self.east)
        self.pull = degree + (mask_even + mask_odd)
        self.rows, self.cols = rows, cols

    def below(self, value):
        return pltpu.roll(value, self.rows - 1, 0)

    def above(self, value):
        return pltpu.roll(value, 1, 0)

    def right(self, value):
        return pltpu.roll(value, self.cols - 1, 1) * self.east

    def left(self, value):
        return pltpu.roll(value, 1, 1) * self.west

    def sample(self, value, flow):
        step = self.right(value) - value
        here = value + flow[1] * step
        lower = self.below(value) + flow[1] * self.below(step)
        return here + flow[0] * (lower - here)

    def inner(self, own):
        total = self.north * self.above(own) + self.south * self.below(own)
        return total + (self.left(own) + self.right(own)) - self.pull * own

    def even(self, value):
        return self.mask_even * self.sample(value, self.flow_even)

    def odd(self, value):
        return self.mask_odd * self.sample(value, self.flow_odd)

    def __call__(self, own, even, odd):
        return self.inner(own) + (self.even(even) + self.odd(odd))

    def bias(self, comp):
        return self.mask_even * self.flow_even[comp] + self.mask_odd * self.flow_odd[comp]


U, V, FE, FO, MK, UE, VE, UO, VO = range(9)


def ring(core, tails, field, c):
    at = 8 * (2 * field + c)
    return jnp.concatenate([core, tails[at : at + 8]], axis=0)


def part(packet, rows, at):
    return packet[rows * at : rows * at + rows]


def stencil_of(ids, nstrips, fe, fo, mk, tails):
    fields = [[ring(x[c], tails, i, c) for c in range(2)] for x, i in ((fe, FE), (fo, FO), (mk, MK))]
    return Stencil(ids[0], nstrips, *fields[:2], *fields[2])


def factors(reset, alpha):
    alpha = jnp.where(reset > 0.5, jnp.float32(0.1), 0.99 * alpha)
    keep = jnp.where(reset > 0.5, jnp.float32(0.0), jnp.float32(1.0))
    return alpha, (1.0 - alpha) * keep, alpha * keep


def gamma():
    return 0.99 * jnp.float32(0.1)


def weights_of(marks):
    weights = []
    for side in range(3):
        alpha = factors(marks[3 * side], jnp.float32(0.1))[0]
        rho = jnp.where(marks[3 * side] > 0.5, jnp.float32(0.0), jnp.float32(1.0))
        weights.append((rho, *factors(marks[3 * side + 1], alpha)[1:]))
    return weights


def start_kernel(resets, pos, vel, out, rs, sems):
    rows = pos.shape[0]
    moves = ((resets, rs), (pos, out.at[pl.ds(0, rows)]), (vel, out.at[pl.ds(rows, rows)]))
    copies = [pltpu.make_async_copy(src, dst, sems.at[i]) for i, (src, dst) in enumerate(moves)]
    for copy in copies:
        copy.start()
    out[2 * rows :] = jnp.zeros((8, out.shape[1]), jnp.float32)
    copies[0].wait()
    for i in range(3):
        mark = jnp.where(rs[i] == 1, jnp.float32(1.0), jnp.float32(0.0))
        out[2 * rows + i : 2 * rows + i + 1] = jnp.full((1, out.shape[1]), mark, jnp.float32)
    for copy in copies[1:]:
        copy.wait()


def rims_kernel(ids, start, fe, fo, mk, even, odd, first, second):
    rows = fe.shape[1]
    comps = [(start, rows * at) for at in range(4)]
    comps += [(x.at[c], 0) for x in (fe, fo, mk) for c in range(2)]
    comps += [(x, rows * at) for x in (even, odd) for at in range(4)]

    def fill(upper, lower):
        at = 0
        for i, (src, base) in enumerate(comps):
            deep = DEEP[i // 2]
            upper[at : at + deep] = src[base : base + deep]
            lower[at : at + deep] = src[base + rows - deep : base + rows]
            at += deep
        for out in (upper, lower):
            out[at:] = jnp.zeros((out.shape[0] - at, out.shape[1]), jnp.float32)

    @pl.when(ids[0] % 2 == 1)
    def _():
        fill(first, second)

    @pl.when(ids[0] % 2 == 0)
    def _():
        fill(second, first)


def first_kernel(nstrips, ids, start, even, odd, fe, fo, mk, second, first, packet, ftails, tails):
    tails[...] = jnp.zeros(tails.shape, jnp.float32)

    def fill(below, above):
        at = 0
        for i in range(2 * len(DEEP)):
            deep = DEEP[i // 2]
            tails[8 * i : 8 * i + deep] = below[at : at + deep]
            tails[8 * i + 8 - deep : 8 * i + 8] = above[at : at + deep]
            at += deep

    @pl.when(ids[0] % 2 == 1)
    def _():
        fill(second, first)

    @pl.when(ids[0] % 2 == 0)
    def _():
        fill(first, second)

    op = stencil_of(ids, nstrips, fe, fo, mk, tails)
    rows = fe.shape[1]
    end = 2 * rows
    packet[end:] = jnp.zeros((8, packet.shape[1]), jnp.float32)
    for c in range(2):
        us = [ring(part(x, rows, c), tails, i, c) for x, i in ((start, U), (even, UE), (odd, UO))]
        f0 = op(*us) + op.bias(c)
        packet[rows * c : rows * c + rows] = f0[:rows]
        ftails[8 * c : 8 * c + 8] = f0[rows:]
        packet[end + 3 * c : end + 3 * c + 2] = f0[rows : rows + 2]
        last = end + (7, 2)[c]
        packet[last : last + 1] = f0[rows + 7 :]


def velocities(start, even, odd, tails, rows, c):
    return [ring(part(x, rows, 2 + c), tails, i, c) for x, i in ((start, V), (even, VE), (odd, VO))]


def beside_kernel(nstrips, ids, marks, start, even, odd, f, ftails, fe, fo, mk, tails, packet, htails, inner):
    op = stencil_of(ids, nstrips, fe, fo, mk, tails)
    rows = fe.shape[1]
    rhos = [w[0] for w in weights_of(marks)]
    packet[2 * rows :] = jnp.zeros((8, packet.shape[1]), jnp.float32)
    for c in range(2):
        h = op(*[rho * x for rho, x in zip(rhos, velocities(start, even, odd, tails, rows, c))])
        packet[rows * c : rows * c + rows] = h[:rows]
        packet[2 * rows + c : 2 * rows + c + 1] = h[rows : rows + 1]
        htails[8 * c : 8 * c + 8] = h[rows:]
        inner[c] = op.inner(rhos[0] * own_ring(f, ftails, rows, c))


def own_ring(packet, tails, rows, c):
    return ring(part(packet, rows, c), tails, 0, c)


def side_ring(packet, rows, c, step):
    tail = packet[2 * rows :]
    tail = pltpu.roll(tail, 8 - step * c, 0) if c else tail
    return jnp.concatenate([part(packet, rows, c), tail], axis=0)


def second_kernel(nstrips, ids, marks, inner, pe, po, fe, fo, mk, tails, packet, gtails):
    op = stencil_of(ids, nstrips, fe, fo, mk, tails)
    rows = mk.shape[1]
    _, rho_even, rho_odd = [w[0] for w in weights_of(marks)]
    packet[2 * rows :] = jnp.zeros((8, packet.shape[1]), jnp.float32)
    for c in range(2):
        even, odd = side_ring(pe, rows, c, 3), side_ring(po, rows, c, 3)
        g = inner[c] + (rho_even * op.even(even) + rho_odd * op.odd(odd))
        packet[rows * c : rows * c + rows] = g[:rows]
        packet[2 * rows + c : 2 * rows + c + 1] = g[rows : rows + 1]
        gtails[8 * c : 8 * c + 8] = g[rows:]


def products(fields, pairs):
    return [fields[i] * fields[j] for i, j in pairs]


def all_pairs(size):
    return [(i, j) for i in range(size) for j in range(i, size)]


EARLY = [(0, 0), (0, 2), (2, 2)]
LATE = [pair for pair in all_pairs(4) if pair not in EARLY]
N_EARLY = 2 + 3 + 3 + 2 * len(EARLY)
N_LATE = 2 * len(LATE)


def tile_sum(value):
    rows = value.shape[0]
    tall = value[0:8]
    for r in range(8, rows, 8):
        tall = tall + value[r : r + 8]
    total = tall[:, 0:128]
    for col in range(128, value.shape[1], 128):
        total = total + tall[:, col : col + 128]
    return total


def lanes_of(totals, at):
    lane = lax.broadcasted_iota(jnp.int32, (1, 128), 1)
    row = jnp.zeros((1, 128), jnp.float32)
    for i, total in enumerate(totals):
        whole = jnp.sum(jnp.sum(total, axis=0, keepdims=True), axis=1, keepdims=True)
        row = jnp.where(lane == at + i, whole, row)
    return row


def gathered(totals, terms):
    parts = [tile_sum(term) for term in terms]
    return parts if totals is None else [x + y for x, y in zip(totals, parts)]


def third_kernel(nstrips, ids, dts, marks, start, even, odd, f, ftails, pe, po, h, htails, he, ho, g, gtails, fe, fo, mk, tails, f2, w2, sums):
    op = stencil_of(ids, nstrips, fe, fo, mk, tails)
    rows = mk.shape[1]
    dt0, dt1, dt2 = dts[0], dts[1], dts[2]
    kappa = 1.0 - gamma()
    weights = weights_of(marks)
    totals = None
    for c in range(2):
        f0s = [own_ring(f, ftails, rows, c), side_ring(pe, rows, c, 3), side_ring(po, rows, c, 3)]
        hs = [own_ring(h, htails, rows, c), side_ring(he, rows, c, 1), side_ring(ho, rows, c, 1)]
        vs = velocities(start, even, odd, tails, rows, c)
        ts = [x + (dt0 * kappa) * y for x, y in zip(f0s, hs)]
        g0 = dt0 * own_ring(g, gtails, rows, c)
        one = [k1 * ((rho * kappa) * v0 + dt1 * t) for v0, t, (rho, k1, _) in zip(vs, ts, weights)]
        mix = [g1 * t for t, (_, _, g1) in zip(ts, weights)]
        rho, k1, g1 = weights[0]
        mu = k1 * (rho * f0s[0] + dt1 * g0)
        both = g1 * g0
        sides = [(w[1] * w[0]) * x for x, w in zip(f0s[1:], weights[1:])]
        forces = [
            ts[0] + dt1 * op(*one),
            g0 + dt1 * op(mu, *sides),
            dt1 * op(*mix),
            dt1 * op.inner(both),
        ]
        forces = [x[:rows] for x in forces]
        kicked = [x[:rows] + dt2 * y for x, y in zip((one[0], mu, mix[0], both), forces)]
        for i in range(4):
            f2[4 * c + i] = forces[i]
            w2[4 * c + i] = kicked[i]
        f0, v0, t, g0 = f0s[0][:rows], vs[0][:rows], ts[0][:rows], g0[:rows]
        terms = products([f0, v0 + dt0 * f0], [(0, 0), (1, 1)]) + products([t, g0], all_pairs(2))
        terms += products([(rho * kappa) * v0 + dt1 * t, rho * f0 + dt1 * g0], all_pairs(2))
        terms += products(forces, EARLY) + products(kicked, EARLY)
        totals = gathered(totals, terms)
    sums[...] = lanes_of(totals, 0)


def fourth_kernel(nstrips, ids, dts, marks, known, w2, early, ge, go, fe, fo, mk, tails, f2, sums):
    op = stencil_of(ids, nstrips, fe, fo, mk, tails)
    rows = known.shape[1]
    dt0, dt1, dt2 = dts[0], dts[1], dts[2]
    weights = weights_of(marks)
    totals = None
    for c in range(2):
        even = op.even(side_ring(ge, rows, c, 1))[:rows]
        odd = op.odd(side_ring(go, rows, c, 1))[:rows]
        scale = dt1 * dt0
        mu = scale * dt1 * (weights[1][1] * even + weights[2][1] * odd)
        both = scale * (weights[1][2] * even + weights[2][2] * odd)
        forces = [known[4 * c], known[4 * c + 1] + mu, known[4 * c + 2], known[4 * c + 3] + both]
        kicked = [w2[4 * c], w2[4 * c + 1] + dt2 * mu, w2[4 * c + 2], w2[4 * c + 3] + dt2 * both]
        f2[2 * c] = forces[1]
        f2[2 * c + 1] = forces[3]
        totals = gathered(totals, products(forces, LATE) + products(kicked, LATE))
    sums[...] = early[...] + lanes_of(totals, N_EARLY)


def form(coefficients, basis):
    total = None
    for (i, j), term in coefficients.items():
        for b in basis[i] + basis[j]:
            term = term * b
        if i != j:
            term = 2.0 * term
        total = term if total is None else total + term
    return jnp.maximum(total, 0.0)


def ratio(kicked, force):
    return jnp.sqrt(kicked / (force + 1e-06))


def last_kernel(dts, marks, parts, start, f, h, g, known, f2, pos, vel, done, sems):
    rows = pos.shape[1]
    copies = []
    sums = jnp.sum(parts[...], axis=0)
    lanes = [sums[:, i : i + 1] for i in range(N_EARLY + N_LATE)]

    def take(pairs, at):
        return {pair: lanes[at + i] for i, pair in enumerate(pairs)}

    dt0, dt1, dt2 = dts[0], dts[1], dts[2]
    kappa = 1.0 - gamma()
    c0 = ratio(lanes[1], lanes[0])
    mu = kappa * dt0 + gamma() * c0
    one = ((), (mu,))
    c1 = ratio(form(take(all_pairs(2), 5), one), form(take(all_pairs(2), 2), one))
    two = ((), (mu,), (c1,), (mu, c1))
    force_sq = take(EARLY, 8) | take(LATE, N_EARLY)
    kicked_sq = take(EARLY, 8 + len(EARLY)) | take(LATE, N_EARLY + len(LATE))
    c2 = ratio(form(kicked_sq, two), form(force_sq, two))
    rho, k1, g1 = weights_of(marks)[0]
    alpha = factors(marks[1], factors(marks[0], jnp.float32(0.1))[0])[0]
    _, k2, g2 = factors(marks[2], alpha)
    for c in range(2):
        f0 = part(f, rows, c)
        speed = rho * (kappa * part(start, rows, 2 + c) + mu * f0)
        field = part(start, rows, c) + dt0 * speed
        force = f0 + (dt0 * kappa) * part(h, rows, c) + (mu * dt0) * part(g, rows, c)
        speed = k1 * (speed + dt1 * force) + (g1 * c1) * force
        field = field + dt1 * speed
        force = known[4 * c] + mu * f2[2 * c] + c1 * (known[4 * c + 2] + mu * f2[2 * c + 1])
        speed = k2 * (speed + dt2 * force) + (g2 * c2) * force
        done[0, c] = field + dt2 * speed
        done[1, c] = speed
        for i, out in enumerate((pos, vel)):
            copies.append(pltpu.make_async_copy(done.at[i, c], out.at[c], sems.at[i, c]))
            copies[-1].start()
    for copy in copies:
        copy.wait()


def call(kernel, out_shape, specs, *args, room=40 * 2**20, out_specs=None, **more):
    return pl.pallas_call(
        kernel,
        out_shape=out_shape,
        in_specs=specs,
        out_specs=out_specs or jax.tree.map(lambda _: VMEM, out_shape),
        compiler_params=pltpu.CompilerParams(vmem_limit_bytes=room),
        **more,
    )(*args)


def f32(*shape):
    return jax.ShapeDtypeStruct(shape, jnp.float32)


def local(positions, velocity, flow_down, flow_up, flow_mask, resets, dt_index):
    nstrips, nz, nx = lax.axis_size("strip"), lax.axis_size("z"), lax.axis_size("x")
    section, strip = lax.axis_index(GZ), lax.axis_index("strip")
    _, comps, rows, cols = positions.shape
    core = f32(comps, rows, cols)
    marks = (resets[:, 0] == 1).astype(jnp.float32)
    start = call(
        start_kernel,
        f32(4 * rows + 8, cols),
        [ANY] * 3,
        resets[:, 0], positions.reshape(-1, cols), velocity.reshape(-1, cols),
        room=None,
        scratch_shapes=[pltpu.SMEM((3,), jnp.int32), pltpu.SemaphoreType.DMA((3,))],
    )
    even, odd = swap(start, GZ, nz * nx)
    marks = jnp.concatenate([marks] + [x[4 * rows : 4 * rows + 3, 0] for x in (even, odd)])
    dts = 0.1 * jnp.power(jnp.float32(1.25), dt_index.astype(jnp.float32))
    ids = jnp.reshape(strip, (1,))
    is_odd = section % 2 == 1
    valid = jnp.stack([section > 0, section < nz * nx - 1]).astype(jnp.int32)
    masks = (flow_mask[:, 0] * valid[:, None, None]).astype(jnp.float32)
    masks = jnp.where(is_odd, masks, masks[::-1])
    flow_even = jnp.where(is_odd, flow_down[0], flow_up[0])
    flow_odd = jnp.where(is_odd, flow_up[0], flow_down[0])
    size = -(-2 * sum(DEEP) // 8) * 8
    rims = call(
        rims_kernel,
        (f32(size, cols), f32(size, cols)),
        [SMEM] + [VMEM] * 6,
        ids, start, flow_even, flow_odd, masks, even, odd,
    )
    first, second = swap(tuple(rims), "strip", nstrips)
    statics = (flow_even, flow_odd, masks)
    side_by_side = pl.CostEstimate(flops=4_000_000, bytes_accessed=3_000_000, transcendentals=0)
    packet = f32(2 * rows + 8, cols)
    ends = (start, even, odd)
    f, ftails, tails = call(
        lambda *refs: first_kernel(nstrips, *refs),
        (packet, f32(16, cols), f32(16 * len(DEEP), cols)),
        [SMEM] + [VMEM] * 8,
        ids, *ends, *statics, second, first,
    )
    pe, po = swap(f, GZ, nz * nx)
    h, htails, inner = call(
        lambda *refs: beside_kernel(nstrips, *refs),
        (packet, f32(16, cols), f32(comps, rows + 8, cols)),
        [SMEM] * 2 + [VMEM] * 9,
        ids, marks, *ends, f, ftails, *statics, tails,
        cost_estimate=side_by_side,
    )
    he, ho = swap(h, GZ, nz * nx)
    g, gtails = call(
        lambda *refs: second_kernel(nstrips, *refs),
        (packet, f32(16, cols)),
        [SMEM] * 2 + [VMEM] * 7,
        ids, marks, inner, pe, po, *statics, tails,
    )
    ge, go = swap(g, GZ, nz * nx)
    known, w2, early = call(
        lambda *refs: third_kernel(nstrips, *refs),
        (f32(4 * comps, rows, cols), f32(4 * comps, rows, cols), f32(1, 128)),
        [SMEM] * 3 + [VMEM] * 17,
        ids, dts, marks, *ends, f, ftails, pe, po, h, htails, he, ho, g, gtails, *statics, tails,
        cost_estimate=side_by_side,
    )
    f2, sums = call(
        lambda *refs: fourth_kernel(nstrips, *refs),
        (f32(2 * comps, rows, cols), f32(1, 128)),
        [SMEM] * 3 + [VMEM] * 9,
        ids, dts, marks, known, w2, early, ge, go, *statics, tails,
    )
    sums = lax.all_to_all(jnp.broadcast_to(sums, (nz, 1, 128)), "z", 0, 0)
    sums = jnp.sum(sums, axis=0)
    near = nx * nstrips
    sums = lax.all_to_all(jnp.broadcast_to(sums, (near, 1, 128)), ("x", "strip"), 0, 0)
    pos, vel = call(
        last_kernel,
        (core, core),
        [SMEM] * 2 + [VMEM] * 7,
        dts, marks, sums, start, f, h, g, known, f2,
        out_specs=(ANY, ANY),
        scratch_shapes=[pltpu.VMEM((2, comps, rows, cols), jnp.float32), pltpu.SemaphoreType.DMA((2, comps))],
    )
    return pos[None], vel[None]


def solution(mesh):
    sections, strips = mesh.devices.shape
    split = mesh.devices.reshape(sections // X_CHIPS, X_CHIPS, strips)
    field = P(GZ, None, "strip", None)
    placed = (field, field, field, field, P(None, GZ, "strip", None), P(None, GZ), P())
    return jax.shard_map(
        local,
        mesh=Mesh(split, ("z", "x", "strip")),
        in_specs=placed,
        out_specs=(field, field),
        check_vma=False,
    )
```
